512 devices in a mesh: sub: 128 (over y, z, core), grp: 4 (over x).
Axes of the slice: x: 4, y: 4, z: 16, core: 2. Of those that a mesh axis runs over, the one named last changes fastest.
Arguments:
- multipliers: float32 [512, 9, 256], P(('sub', 'grp')), may hold values from -6 to 6
- residual: float32 [512, 9, 256], P(('sub', 'grp')), may hold values from -6 to 6
- stiff_class: int32 [512, 16, 256], P(('sub', 'grp')), may hold values from 0 to 7
- moduli: float32 [8], replicated, may hold values from 1 to 30
- coarse_panel: float32 [512, 24, 96], P(('sub', 'grp')), as said below
Outputs:
- new_multipliers: float32 [512, 9, 256], P(('sub', 'grp'))
- new_residual: float32 [512, 9, 256], P(('sub', 'grp'))
The draws below stay inside these ranges and needn't reach their ends.
Inputs may be any that keep to these rules, and one draw needn't show every extreme that they name: `coarse_panel`: for each s, the panels of the 4 subdomains s * 4 + g stacked in order of g form a symmetric positive definite matrix of 96 rows.
All inputs are finite; a program needn't handle non-finite values.
Results may differ from the reference program's by a relative error of at most 0.0003.
Values sent between devices are 32-bit elements; how exact they have to be, the bound alone decides.
A program may use at most 64 MiB of HBM per device.

```python
import math
import jax
import jax.numpy as jnp
from jax import lax

EDGE = 16
SPAN = 4
ITERS = 2
PRE_SWEEPS = 2
POST_SWEEPS = 2
COARSE_SWEEPS = 4
NCLASS = 8
CORNER_DOFS = 24
GROUP_DOFS = 96
DOMAINS = 512
N_SUB = 128
N_GRP = 4


panel_level = 1500.0


def draw_coarse_panel(key, part):
    first_key, second_key = jax.random.split(key, 2)
    base = jax.random.uniform(first_key, (N_SUB, GROUP_DOFS, GROUP_DOFS), jnp.float32, -1.0, 1.0)
    symmetric = (base + jnp.swapaxes(base, 1, 2)) / (2.0 * GROUP_DOFS)
    diagonal = 1.0 + jax.random.uniform(second_key, (N_SUB, GROUP_DOFS), jnp.float32, 0.0, 1.0)
    identity = jnp.eye(GROUP_DOFS, dtype=jnp.float32)
    matrix = panel_level * (symmetric * (1.0 - identity) + diagonal[:, :, None] * identity)
    return matrix.reshape(N_SUB * N_GRP, CORNER_DOFS, GROUP_DOFS)


def plant(values, rng, smallest, largest):
    longest = values.shape.index(max(values.shape))
    spots = []
    for shift in (0, 1):
        where = [jax.random.randint(jax.random.fold_in(rng, axis), (), 0, length) for axis, length in enumerate(values.shape)]
        where[longest] = (where[longest] + shift) % values.shape[longest]
        spots.append(tuple(where))
    return values.at[spots[0]].set(smallest).at[spots[1]].set(largest)


def steps_of(key, shape, cuts, least, largest):
    def one(dim, blocks):
        steps = jax.random.uniform(jax.random.fold_in(jax.random.fold_in(key, 6), dim), (blocks,), jnp.float32, least / len(cuts), largest / len(cuts))
        return jnp.repeat(jnp.exp(steps), shape[dim] // blocks).reshape((-1,) + (1,) * (len(shape) - dim - 1))

    factor_of = one(*cuts[0])
    for cut in cuts[1:]:
        factor_of = factor_of * one(*cut)
    return factor_of


def noise(own_key, extent, scale, reach, cuts=(), held_as=jnp.bfloat16):
    loudness = steps_of(own_key, extent, cuts, -0.22, 0.18) if cuts else 1.0
    values = jax.random.normal(own_key, extent, jnp.float32) * scale * loudness
    return jnp.minimum(jnp.maximum(values, -reach), reach).astype(held_as)


def setup_inputs(seed: int = 0) -> dict:
    keys = jax.random.split(jax.random.key(seed), 6)
    return {
        "multipliers": noise(keys[0], (DOMAINS, 9, EDGE * EDGE), 1.0, 6.0, ((0, 512),), jnp.float32),
        "residual": noise(keys[1], (DOMAINS, 9, EDGE * EDGE), 1.0, 6.0, ((0, 512),), jnp.float32),
        "stiff_class": plant(jax.random.randint(keys[2], (DOMAINS, EDGE, EDGE * EDGE), 0, NCLASS), jax.random.fold_in(keys[2], 1), 0, NCLASS - 1).astype(jnp.int32),
        "moduli": jnp.clip(jnp.exp(jax.random.uniform(keys[3], (NCLASS,), jnp.float32, math.log(1.0), math.log(30.0))), 1.0, 30.0),
        "coarse_panel": draw_coarse_panel(jax.random.fold_in(keys[5], 71), 0),
    }


mass_weight = 0.5
damping = 0.8

def build_operator(stiffness, mass_scale, edge_scale):
    weight_x = edge_scale * 0.5 * (stiffness[1:] + stiffness[:-1])
    weight_y = edge_scale * 0.5 * (stiffness[:, 1:] + stiffness[:, :-1])
    weight_z = edge_scale * 0.5 * (stiffness[:, :, 1:] + stiffness[:, :, :-1])
    mass_term = mass_scale * stiffness
    diagonal = mass_term + jnp.pad(weight_x, ((0, 1), (0, 0), (0, 0))) + jnp.pad(weight_x, ((1, 0), (0, 0), (0, 0)))
    diagonal = diagonal + jnp.pad(weight_y, ((0, 0), (0, 1), (0, 0))) + jnp.pad(weight_y, ((0, 0), (1, 0), (0, 0)))
    diagonal = diagonal + jnp.pad(weight_z, ((0, 0), (0, 0), (0, 1))) + jnp.pad(weight_z, ((0, 0), (0, 0), (1, 0)))
    return (mass_term, weight_x, weight_y, weight_z, diagonal)

def apply_operator(operator, nodal):
    mass_term, weight_x, weight_y, weight_z, diagonal = operator
    flux_x = weight_x * (nodal[:, 1:] - nodal[:, :-1])
    flux_y = weight_y * (nodal[:, :, 1:] - nodal[:, :, :-1])
    flux_z = weight_z * (nodal[:, :, :, 1:] - nodal[:, :, :, :-1])
    result = mass_term * nodal
    result = result + jnp.pad(flux_x, ((0, 0), (1, 0), (0, 0), (0, 0))) - jnp.pad(flux_x, ((0, 0), (0, 1), (0, 0), (0, 0)))
    result = result + jnp.pad(flux_y, ((0, 0), (0, 0), (1, 0), (0, 0))) - jnp.pad(flux_y, ((0, 0), (0, 0), (0, 1), (0, 0)))
    result = result + jnp.pad(flux_z, ((0, 0), (0, 0), (0, 0), (1, 0))) - jnp.pad(flux_z, ((0, 0), (0, 0), (0, 0), (0, 1)))
    return result

def coarsen(values):
    half_nodes = values.shape[-1] // 2
    leading = values.shape[:-3]
    shaped = values.reshape(leading + (half_nodes, 2, half_nodes, 2, half_nodes, 2))
    return shaped.sum(axis=(-5, -3, -1))

def refine(values):
    half_nodes = values.shape[-1]
    leading = values.shape[:-3]
    expanded = values[..., :, None, :, None, :, None]
    expanded = jnp.broadcast_to(expanded, leading + (half_nodes, 2, half_nodes, 2, half_nodes, 2))
    return expanded.reshape(leading + (2 * half_nodes, 2 * half_nodes, 2 * half_nodes))

def vcycle(fine_op, coarse_op, source):
    fine_diag = fine_op[4]
    coarse_diag = coarse_op[4]
    solution = damping * source / fine_diag
    for sweep_index in range(PRE_SWEEPS - 1):
        solution = solution + damping * (source - apply_operator(fine_op, solution)) / fine_diag
    defect = coarsen(source - apply_operator(fine_op, solution))
    correction = damping * defect / coarse_diag
    for sweep_index in range(COARSE_SWEEPS - 1):
        correction = correction + damping * (defect - apply_operator(coarse_op, correction)) / coarse_diag
    solution = solution + refine(correction)
    for sweep_index in range(POST_SWEEPS):
        solution = solution + damping * (source - apply_operator(fine_op, solution)) / fine_diag
    return solution

def corner_table(side_nodes):
    slope = jnp.arange(side_nodes).astype(jnp.float32) / (side_nodes - 1)
    return jnp.stack([1.0 - slope, slope])

def corner_sums(nodal, corner_ramp):
    summed = jnp.einsum('cijl,ai,bj,el->cabe', nodal, corner_ramp, corner_ramp, corner_ramp, precision=lax.Precision.HIGHEST)
    return summed.reshape(CORNER_DOFS)

def corner_spread(values, corner_ramp):
    shaped = values.reshape(3, 2, 2, 2)
    return jnp.einsum('cabe,ai,bj,el->cijl', shaped, corner_ramp, corner_ramp, corner_ramp, precision=lax.Precision.HIGHEST)

def spread_faces(own_faces, lower_faces):
    side_nodes = own_faces.shape[-1]
    nodal = jnp.zeros((3, side_nodes, side_nodes, side_nodes), jnp.float32)
    nodal = nodal.at[:, side_nodes - 1, :, :].add(own_faces[0]).at[:, 0, :, :].add(-lower_faces[0])
    nodal = nodal.at[:, :, side_nodes - 1, :].add(own_faces[1]).at[:, :, 0, :].add(-lower_faces[1])
    nodal = nodal.at[:, :, :, side_nodes - 1].add(own_faces[2]).at[:, :, :, 0].add(-lower_faces[2])
    return nodal

def face_layers(nodal):
    low_layer = jnp.stack([nodal[:, 0], nodal[:, :, 0], nodal[:, :, :, 0]])
    high_layer = jnp.stack([nodal[:, -1], nodal[:, :, -1], nodal[:, :, :, -1]])
    return (low_layer, high_layer)

def cholesky_solve(factor, group_rhs):
    column = group_rhs[:, None]
    middle = lax.linalg.triangular_solve(factor, column, left_side=True, lower=True)
    solved = lax.linalg.triangular_solve(factor, middle, left_side=True, lower=True, transpose_a=True)
    return solved[:, 0]

def reference(multipliers, residual, stiff_class, moduli, coarse_panel):
    domains = stiff_class.shape[0]
    side_nodes = stiff_class.shape[1]
    numbering = jnp.arange(domains)
    member = numbering % N_GRP
    block_index = numbering // N_GRP
    grid_row = block_index // SPAN
    grid_col = block_index % SPAN
    upper_ok = jnp.stack([grid_row < N_SUB // SPAN - 1, grid_col < SPAN - 1, member < N_GRP - 1], axis=1)
    upper_ok = upper_ok.astype(jnp.float32)[:, :, None, None, None]
    lower_ok = jnp.stack([grid_row > 0, grid_col > 0, member > 0], axis=1)
    lower_ok = lower_ok.astype(jnp.float32)[:, :, None, None, None]
    strides = (SPAN * N_GRP, N_GRP, 1)
    corner_ramp = corner_table(side_nodes)

    def from_lower(faces):
        moved = [jnp.roll(faces[:, direction], strides[direction], axis=0) for direction in range(3)]
        return jnp.stack(moved, axis=1) * lower_ok

    def from_upper(faces):
        moved = [jnp.roll(faces[:, direction], -strides[direction], axis=0) for direction in range(3)]
        return jnp.stack(moved, axis=1) * upper_ok

    def operators(classes):
        stiffness = moduli[classes.reshape(side_nodes, side_nodes, side_nodes)]
        fine_op = build_operator(stiffness, mass_weight, 1.0)
        coarse_op = build_operator(coarsen(stiffness) / 8.0, 8.0 * mass_weight, 4.0)
        return (fine_op, coarse_op)

    def precondition(misfit):
        lower_faces = from_lower(misfit)

        def local_apply(pieces):
            own_faces, below_faces, classes = pieces
            fine_op, coarse_op = operators(classes)
            return face_layers(apply_operator(fine_op, spread_faces(own_faces, below_faces)))
        low_layer, high_layer = lax.map(local_apply, (misfit, lower_faces, stiff_class))
        return 0.25 * (high_layer - from_upper(low_layer)) * upper_ok
    group_matrix = coarse_panel.reshape(N_SUB, GROUP_DOFS, GROUP_DOFS)
    factors = jnp.linalg.cholesky(group_matrix)

    def dual_apply(direction):
        lower_faces = from_lower(direction)

        def local_solve(pieces):
            own_faces, below_faces, classes = pieces
            fine_op, coarse_op = operators(classes)
            source = spread_faces(own_faces, below_faces)
            smooth = vcycle(fine_op, coarse_op, source)
            low_layer, high_layer = face_layers(smooth)
            return (low_layer, high_layer, corner_sums(source, corner_ramp))
        low_layer, high_layer, corners = lax.map(local_solve, (direction, lower_faces, stiff_class))
        group_rhs = corners.reshape(N_SUB, GROUP_DOFS)
        solved = jax.vmap(cholesky_solve)(factors, group_rhs).reshape(domains, CORNER_DOFS)

        def spread_local(values):
            return face_layers(corner_spread(values, corner_ramp))
        low_extra, high_extra = lax.map(spread_local, solved)
        low_layer = low_layer + low_extra
        high_layer = high_layer + high_extra
        return (high_layer - from_upper(low_layer)) * upper_ok
    dual_values = multipliers.reshape(domains, 3, 3, side_nodes, side_nodes) * upper_ok
    misfit = residual.reshape(domains, 3, 3, side_nodes, side_nodes) * upper_ok
    inner_old = jnp.float32(1.0)
    direction = misfit
    for step_index in range(ITERS):
        smoothed = precondition(misfit)
        precond_inner = jnp.sum(misfit * smoothed)
        if step_index == 0:
            direction = smoothed
        else:
            direction = smoothed + precond_inner / inner_old * direction
        applied = dual_apply(direction)
        step_size = precond_inner / jnp.sum(direction * applied)
        dual_values = dual_values + step_size * direction
        misfit = misfit - step_size * applied
        inner_old = precond_inner
    shape_out = (domains, 9, side_nodes * side_nodes)
    return (dual_values.reshape(shape_out), misfit.reshape(shape_out))
```

```python
import functools

import jax
import jax.numpy as jnp
from jax import lax
from jax.experimental import pallas as pl
from jax.experimental.pallas import tpu as pltpu
from jax.sharding import PartitionSpec as P

MESH = pl.DeviceIdType.MESH
F32 = jnp.float32
SPAN = 4
CORNER = 24
DAMP = 0.8
HI = lax.Precision.HIGHEST


def roll(x, shift, axis):
    shift = shift % x.shape[axis]
    return x if shift == 0 else pltpu.roll(x, shift, axis)


def iota(shape, axis):
    return lax.broadcasted_iota(jnp.int32, shape, axis)


def m3(coef, field):
    return (field.reshape(3, 16, 256) * coef[None]).reshape(48, 256)


def neighbours(v, k):
    return (
        roll(v, -k, 0),
        roll(v, k, 0),
        roll(v, -16 * k, 1),
        roll(v, 16 * k, 1),
        roll(v, -k, 1),
        roll(v, k, 1),
    )


def weighted(coefs, v, k):
    terms = [m3(a, n) for a, n in zip(coefs, neighbours(v, k))]
    return (terms[0] + terms[1]) + (terms[2] + terms[3]) + (terms[4] + terms[5])


def pair_sum(v):
    rows, lanes = iota(v.shape, 0), iota(v.shape, 1)
    v = v + jnp.where(rows % 2 == 0, roll(v, -1, 0), roll(v, 1, 0))
    v = v + jnp.where(lanes % 32 < 16, roll(v, -16, 1), roll(v, 16, 1))
    return v + jnp.where(lanes % 2 == 0, roll(v, -1, 1), roll(v, 1, 1))


def edge_weights(s, k, scale):
    rows, lanes = iota(s.shape, 0), iota(s.shape, 1)
    coordinate = (rows, lanes // 16, lanes % 16)
    shifts = ((k, 0), (16 * k, 1), (k, 1))
    weights = []
    for where, (step, axis) in zip(coordinate, shifts):
        up = jnp.where(where < 16 - k, scale * (s + roll(s, -step, axis)), 0.0)
        low = jnp.where(where >= k, scale * (s + roll(s, step, axis)), 0.0)
        weights += [up, low]
    return weights, sum(weights[1:], weights[0])


def place(own, low):
    lane = iota((16, 128), 1)
    row = iota((16, 128), 0)
    inner = lane % 16
    parts = []
    for c in range(3):
        halves = []
        for h in range(2):
            r = 3 * h + c
            t = jnp.where(row == 15, own[r : r + 1, :], 0.0)
            t = t - jnp.where(row == 0, low[r : r + 1, :], 0.0)
            if h == 1:
                t = t + jnp.where(lane >= 112, roll(own[8:24], -16 - 16 * c, 1), 0.0)
            else:
                t = t - jnp.where(lane < 16, roll(low[8:24], -16 * c, 1), 0.0)
            t = t + jnp.where(inner == 15, roll(own[24:40], 15 - c - 3 * h, 1), 0.0)
            t = t - jnp.where(inner == 0, roll(low[24:40], -c - 3 * h, 1), 0.0)
            halves.append(t)
        parts.append(jnp.concatenate(halves, axis=1))
    return jnp.concatenate(parts, axis=0)


def pack(v, buf, high):
    lane = iota((16, 128), 1)
    inner = lane % 16
    at = 15 if high else 0
    y = z = None
    for c in range(3):
        for h in range(2):
            r = 3 * h + c
            part = v[16 * c : 16 * c + 16, 128 * h : 128 * h + 128]
            buf[r : r + 1, :] = part[at : at + 1, :]
            t = roll(jnp.where(inner == at, part, 0.0), c + 3 * h - at, 1)
            z = t if z is None else z + t
        if high:
            part = v[16 * c : 16 * c + 16, 128:256]
            t = roll(jnp.where(lane >= 112, part, 0.0), 16 + 16 * c, 1)
        else:
            part = v[16 * c : 16 * c + 16, 0:128]
            t = roll(jnp.where(lane < 16, part, 0.0), 16 * c, 1)
        y = t if y is None else y + t
    buf[6:8, :] = jnp.zeros((2, 128), F32)
    buf[8:24, :] = y
    buf[24:40, :] = z


def from_rows(rows, buf):
    lane = iota((16, 256), 1)
    row = iota((16, 256), 0)
    m, n = iota((256, 128), 0) % 16, iota((256, 128), 1)
    to_y = jnp.where(m == n % 16, 1.0, 0.0)
    to_z = jnp.where(n == (m % 8) * 16 + 3 * (m // 8), 1.0, 0.0)

    def spread(first):
        return jnp.concatenate(
            [jnp.where(lane // 16 == row, rows[first + c : first + c + 1, :], 0.0) for c in range(3)],
            axis=0,
        )

    y = jnp.dot(spread(3), to_y, precision=HI, preferred_element_type=F32)
    z = jnp.dot(spread(6), to_z, precision=HI, preferred_element_type=F32)
    group = iota((16, 128), 1) // 16
    buf[0:3, :] = rows[0:3, 0:128]
    buf[3:6, :] = rows[0:3, 128:256]
    buf[6:8, :] = jnp.zeros((2, 128), F32)
    buf[8:24, :] = sum(jnp.where(group == c, y[16 * c : 16 * c + 16], 0.0) for c in range(3))
    buf[24:40, :] = sum(roll(z[16 * c : 16 * c + 16], c, 1) for c in range(3))


def to_rows(faces, buf, slot):
    lane = iota((16, 256), 1)
    row = iota((16, 256), 0)
    n, m = iota((128, 256), 0), iota((128, 256), 1) % 16
    from_y = jnp.where(n == m, 1.0, 0.0)
    from_z = jnp.where(n == (m % 8) * 16 + 3 * (m // 8), 1.0, 0.0)
    y = jnp.concatenate([roll(faces[8:24], -16 * c, 1) for c in range(3)], axis=0)
    z = jnp.concatenate([roll(faces[24:40], -c, 1) for c in range(3)], axis=0)
    y = jnp.dot(y, from_y, precision=HI, preferred_element_type=F32)
    z = jnp.dot(z, from_z, precision=HI, preferred_element_type=F32)
    buf[slot, 0:3, 0:128] = faces[0:3]
    buf[slot, 0:3, 128:256] = faces[3:6]
    for c in range(3):
        for first, t in ((3, y), (6, z)):
            t = jnp.where(lane // 16 == row, t[16 * c : 16 * c + 16], 0.0)
            buf[slot, first + c : first + c + 1, :] = jnp.sum(t, axis=0, keepdims=True)


def partial_dot(a, b):
    t = jnp.sum(a * b, axis=0, keepdims=True)
    return t[:, 0:128] + t[:, 128:256]


def eliminate(first, last, matrix):
    size = matrix.shape[0]
    row_a, lane_a = iota((size, 128), 0), iota((size, 128), 1)
    row_b, lane_b = iota((8, 128), 0), iota((8, 128), 1)
    lane_w = iota((1, 128), 1)

    def block(k, a):
        matrix[...] = a
        base = pl.multiple_of(k * 8, 8)
        b = matrix[pl.ds(base, 8), :]
        local_a = row_a - base
        for t in range(0, 8, 2):
            r0, r1 = b[t : t + 1, :], b[t + 1 : t + 2, :]
            p, q, s = r0[:, t : t + 1], r0[:, t + 1 : t + 2], r1[:, t + 1 : t + 2]
            inverse = 1.0 / (p * s - q * q)
            p, q, s = p * inverse, q * inverse, s * inverse
            w0, w1 = s * r0 - q * r1, p * r1 - q * r0
            w0 = jnp.where(lane_w == t, s, jnp.where(lane_w == t + 1, -q, w0))
            w1 = jnp.where(lane_w == t, -q, jnp.where(lane_w == t + 1, p, w1))

            def update(x, row, lane):
                rows = x.shape[0]
                column = row[:, 0:1]
                c0 = jnp.where(column == t, -1.0, jnp.where(column == t + 1, 0.0, x[:, t : t + 1]))
                c1 = jnp.where(column == t, 0.0, jnp.where(column == t + 1, -1.0, x[:, t + 1 : t + 2]))
                hit = (row == t) | (row == t + 1) | (lane == t) | (lane == t + 1)
                return jnp.where(hit, 0.0, x) - c0 * w0 - c1 * w1

            a, b = update(a, local_a, lane_a), update(b, row_b, lane_b)
        return roll(a, -8, 1)

    matrix[...] = lax.fori_loop(first, last, block, matrix[...])


def kernel(
    G, Y, Z, mult_ref, res_ref, class_ref, moduli_ref, panel_ref, lam_ref, out_ref,
    matrix, panel, sent_hi, sent_lo, got_hi, got_lo, corner_out, corner_in,
    tiles, x_in, yc_in, z_in, rows, send_sem, recv_sem,
):
    sub, member = lax.axis_index("sub"), lax.axis_index("grp")
    n_sub = Y * Z * 2
    grid_row, grid_col = sub // SPAN, sub % SPAN
    upper = (
        ((sub + SPAN) % n_sub, member),
        (grid_row * SPAN + (grid_col + 1) % SPAN, member),
        (sub, (member + 1) % G),
    )
    lower = (
        ((sub + n_sub - SPAN) % n_sub, member),
        (grid_row * SPAN + (grid_col + SPAN - 1) % SPAN, member),
        (sub, (member + G - 1) % G),
    )
    upper_ok = [
        (grid_row < n_sub // SPAN - 1).astype(F32),
        (grid_col < SPAN - 1).astype(F32),
        (member < G - 1).astype(F32),
    ]
    lower_ok = [
        (grid_row > 0).astype(F32),
        (grid_col > 0).astype(F32),
        (member > 0).astype(F32),
    ]
    core, z, y = sub % 2, (sub // 2) % Z, sub // (2 * Z)
    by_distance = lambda n: sorted(range(1, n), key=lambda i: -min(i, n - i))
    x_partners = [(sub, (member + i) % G) for i in by_distance(G)]
    yc_partners = [
        (((y + i) % Y * Z + z) * 2 + (core + c) % 2, member)
        for i in by_distance(Y) + [0]
        for c in (1, 0)
        if (i, c) != (0, 0)
    ]
    z_partners = [((y * Z + (z + i) % Z) * 2 + core, member) for i in by_distance(Z)]

    barrier = pltpu.get_barrier_semaphore()
    greeted = z_partners + list(upper) + list(lower) + yc_partners + x_partners
    for device in greeted:
        pl.semaphore_signal(barrier, inc=1, device_id=device, device_id_type=MESH)

    copies = []

    def send(src, dst, device):
        i = len(copies)
        copy = pltpu.make_async_remote_copy(
            src_ref=src, dst_ref=dst, send_sem=send_sem.at[i], recv_sem=recv_sem.at[i],
            device_id=device, device_id_type=MESH,
        )
        copy.start()
        copies.append(copy)
        return copy

    def wait(group):
        for copy in group:
            copy.wait_recv()

    spans = ((0, 8), (8, 24), (24, 40))
    order = (0, 2, 1)

    def exchange(e, both=True, up=True):
        group = []
        for k in order:
            first, last = spans[k]
            if up:
                group.append(
                    send(sent_hi.at[e, first:last], got_hi.at[e, first:last], upper[k])
                )
            if both:
                group.append(
                    send(sent_lo.at[e, first:last], got_lo.at[e, first:last], lower[k])
                )
        return group

    face_row = iota((40, 128), 0)

    def face_mask(ok):
        return jnp.where(face_row < 8, ok[0], jnp.where(face_row < 24, ok[1], ok[2]))

    up_mask, low_mask = face_mask(upper_ok), face_mask(lower_ok)
    row9 = iota((9, 256), 0)
    row_mask = jnp.where(
        row9 < 3, upper_ok[0], jnp.where(row9 < 6, upper_ok[1], upper_ok[2])
    )

    size = G * CORNER
    own_rows = pl.ds(pl.multiple_of(member * CORNER, 8), CORNER)
    panel[...] = jnp.zeros((CORNER, 128), F32)
    panel[:, 0:size] = panel_ref[0]
    matrix[own_rows, :] = panel[...]

    residual = res_ref[0] * row_mask
    from_rows(residual, sent_hi.at[0])
    rows[0] = residual

    classes = class_ref[0]
    stiffness = jnp.zeros((16, 256), F32)
    for level in range(8):
        stiffness = stiffness + jnp.where(classes == level, moduli_ref[level], 0.0)
    weight, total = edge_weights(stiffness, 1, 0.5)
    diagonal = 0.5 * stiffness + total
    scale = DAMP / diagonal
    relax = [scale * w for w in weight]
    block_mean = pair_sum(stiffness) * 0.125
    coarse_weight, coarse_total = edge_weights(block_mean, 2, 2.0)
    coarse_scale = DAMP / (4.0 * block_mean + coarse_total)
    coarse_relax = [coarse_scale * w for w in coarse_weight]

    def operator(v):
        return m3(diagonal, v) - weighted(weight, v, 1)

    def vcycle(f):
        g = m3(scale, f)
        v = g
        v = (1.0 - DAMP) * v + g + weighted(relax, v, 1)
        h = m3(coarse_scale, pair_sum(f - operator(v)))
        e = h
        for _ in range(3):
            e = (1.0 - DAMP) * e + h + weighted(coarse_relax, e, 2)
        v = v + e
        for _ in range(2):
            v = (1.0 - DAMP) * v + g + weighted(relax, v, 1)
        return v

    lanes = iota((1, 256), 1)
    ramp_y = (lanes // 16).astype(F32) / 15.0
    ramp_z = (lanes % 16).astype(F32) / 15.0
    plane = [
        by * bz for by in (1.0 - ramp_y, ramp_y) for bz in (1.0 - ramp_z, ramp_z)
    ]
    ramp_x = iota((16, 256), 0).astype(F32) / 15.0
    row8, lane8 = iota((8, 128), 0), iota((8, 128), 1)
    row8w = iota((8, 256), 0)
    plane8 = sum(jnp.where(row8w % 4 == n, plane[n], 0.0) for n in range(4))

    def corner_sums(f):
        t = jnp.zeros((8, 256), F32)
        for c in range(3):
            part = f[16 * c : 16 * c + 16]
            for a, ramp in ((0, 1.0 - ramp_x), (1, ramp_x)):
                line = jnp.sum(part * ramp, axis=0, keepdims=True)
                t = t + jnp.where(row8w == 2 * c + a, line, 0.0)
        result = jnp.zeros((8, 128), F32)
        for n in range(4):
            s = t * plane[n]
            s = jnp.sum(s[:, 0:128] + s[:, 128:256], axis=1, keepdims=True)
            at = (lane8 == member * CORNER + row8 * 4 + n) & (row8 < 6)
            result = result + jnp.where(at, s, 0.0)
        return result

    def corner_send(e, f):
        corner_out[e] = corner_sums(f)
        return [
            send(corner_out.at[e], corner_in.at[e, i], device)
            for i, device in enumerate(x_partners)
        ]

    def corner_field(e):
        rhs = corner_out[e]
        for i in range(G - 1):
            rhs = rhs + corner_in[e, i]
        rhs = jnp.sum(rhs, axis=0, keepdims=True)
        solved = jnp.sum(matrix[own_rows, :] * rhs, axis=1, keepdims=True)
        parts = []
        for c in range(3):
            t = solved[8 * c : 8 * c + 8] * plane8
            t0 = jnp.sum(jnp.where(row8w < 4, t, 0.0), axis=0, keepdims=True)
            t1 = jnp.sum(jnp.where(row8w >= 4, t, 0.0), axis=0, keepdims=True)
            parts.append((1.0 - ramp_x) * t0 + ramp_x * t1)
        return jnp.concatenate(parts, axis=0)

    pl.semaphore_wait(barrier, len(greeted))

    group = exchange(0, both=False)
    panels = [send(panel, matrix.at[own_rows, :], device) for device in x_partners]
    wait(group)
    f_r = place(sent_hi[0], got_hi[0] * low_mask)

    image = operator(f_r)
    pack(image, sent_hi.at[1], True)
    pack(image, sent_lo.at[1], False)
    group = exchange(1)
    dots = [0.25 * partial_dot(f_r, image)]
    wait(panels)
    half = size // 16
    eliminate(0, half, matrix)
    wait(group)
    u = (sent_hi[1] - got_lo[1]) * (0.25 * up_mask)
    f_u = place(u, (got_hi[1] - sent_lo[1]) * (0.25 * low_mask))

    group = corner_send(0, f_u)
    v = vcycle(f_u)
    eliminate(half, 2 * half, matrix)
    matrix[...] = roll(matrix[...], size - 128, 1)
    wait(group)
    v = v + corner_field(0)
    pack(v, sent_hi.at[2], True)
    pack(v, sent_lo.at[2], False)
    group = exchange(2)
    dots.append(partial_dot(f_u, v))
    to_rows(u, rows, 1)
    wait(group)
    q = (sent_hi[2] - got_lo[2]) * up_mask
    f_q = place(q, (got_hi[2] - sent_lo[2]) * low_mask)

    image = operator(f_q)
    pack(image, sent_hi.at[3], True)
    pack(image, sent_lo.at[3], False)
    group = exchange(3)
    dots.append(0.25 * partial_dot(f_r, image))
    dots.append(0.25 * partial_dot(f_q, image))
    to_rows(q, rows, 2)
    wait(group)
    w = (sent_hi[3] - got_lo[3]) * (0.25 * up_mask)
    f_w = place(w, (got_hi[3] - sent_lo[3]) * (0.25 * low_mask))

    group = corner_send(1, f_w)
    v = vcycle(f_w)
    wait(group)
    v = v + corner_field(1)
    dots.append(partial_dot(f_u, v))
    dots.append(partial_dot(f_w, v))

    tile = jnp.zeros((8, 128), F32)
    for i, d in enumerate(dots):
        tile = tile + jnp.where(row8 == i, d, 0.0)

    def spread(slot, landing, partners):
        tiles[slot] = tile
        return [
            send(tiles.at[slot], landing.at[i], device) for i, device in enumerate(partners)
        ]

    def collect(group, landing):
        wait(group)
        total = tile
        for i in range(landing.shape[0]):
            total = total + landing[i]
        return total

    group = spread(0, x_in, x_partners)
    pack(v, sent_hi.at[4], True)
    pack(v, sent_lo.at[4], False)
    last = exchange(4, up=False)
    to_rows(w, rows, 3)
    tile = collect(group, x_in)
    group = spread(1, yc_in, yc_partners)
    wait(last)
    to_rows((sent_hi[4] - got_lo[4]) * up_mask, rows, 4)
    tile = collect(group, yc_in)
    group = spread(2, z_in, z_partners)
    tile = collect(group, z_in)

    sums = jnp.sum(tile, axis=1, keepdims=True)
    ru, uq, rw, qw, us, ws = [sums[i : i + 1, :] for i in range(6)]
    a = ru / uq
    next_inner = ru - a * (rw + uq) + a * a * qw
    c = 1.0 + next_inner / ru
    curve = c * c * uq - c * a * (us + qw) + a * a * ws
    b = next_inner / curve
    first, second = a + b * c, a * b
    lam_ref[0] = mult_ref[0] * row_mask + first * rows[1] - second * rows[3]
    out_ref[0] = rows[0] - first * rows[2] + second * rows[4]
    for copy in copies:
        copy.wait_send()


def solution(mesh):
    G, n_sub = mesh.shape["grp"], mesh.shape["sub"]
    Z = min(16, n_sub // 2)
    Y = n_sub // (2 * Z)
    size = G * CORNER
    copies = 3 + 3 * 6 + 3 + 4 * (G - 1) + (2 * Y - 1) + (Z - 1)

    def per_device(multipliers, residual, stiff_class, moduli, coarse_panel):
        vmem = pl.BlockSpec(memory_space=pltpu.VMEM)
        return pl.pallas_call(
            functools.partial(kernel, G, Y, Z),
            out_shape=[jax.ShapeDtypeStruct((1, 9, 256), F32)] * 2,
            in_specs=[vmem, vmem, vmem, pl.BlockSpec(memory_space=pltpu.SMEM), vmem],
            out_specs=[vmem, vmem],
            scratch_shapes=[
                pltpu.VMEM((size, 128), F32),
                pltpu.VMEM((CORNER, 128), F32),
                pltpu.VMEM((5, 40, 128), F32),
                pltpu.VMEM((5, 40, 128), F32),
                pltpu.VMEM((5, 40, 128), F32),
                pltpu.VMEM((5, 40, 128), F32),
                pltpu.VMEM((2, 8, 128), F32),
                pltpu.VMEM((2, G - 1, 8, 128), F32),
                pltpu.VMEM((3, 8, 128), F32),
                pltpu.VMEM((G - 1, 8, 128), F32),
                pltpu.VMEM((2 * Y - 1, 8, 128), F32),
                pltpu.VMEM((Z - 1, 8, 128), F32),
                pltpu.VMEM((5, 9, 256), F32),
                pltpu.SemaphoreType.DMA((copies,)),
                pltpu.SemaphoreType.DMA((copies,)),
            ],
            compiler_params=pltpu.CompilerParams(
                collective_id=0, has_side_effects=True, vmem_limit_bytes=32 * 1024 * 1024
            ),
            name="feti",
        )(multipliers, residual, stiff_class, moduli, coarse_panel)

    device = P(("sub", "grp"), None, None)
    return jax.shard_map(
        per_device,
        mesh=mesh,
        in_specs=(device, device, device, P(), device),
        out_specs=(device, device),
        check_vma=False,
    )
```

```python
import functools

import jax
import jax.numpy as jnp
from jax import lax
from jax.experimental import pallas as pl
from jax.experimental.pallas import tpu as pltpu
from jax.sharding import PartitionSpec as P

MESH = pl.DeviceIdType.MESH
F32 = jnp.float32
SPAN = 4
CORNER = 24
DAMP = 0.8
HI = lax.Precision.HIGHEST


def roll(x, shift, axis):
    shift = shift % x.shape[axis]
    return x if shift == 0 else pltpu.roll(x, shift, axis)


def iota(shape, axis):
    return lax.broadcasted_iota(jnp.int32, shape, axis)


def m3(coef, field):
    return (field.reshape(3, 16, 256) * coef[None]).reshape(48, 256)


def neighbours(v, k):
    return (
        roll(v, -k, 0),
        roll(v, k, 0),
        roll(v, -16 * k, 1),
        roll(v, 16 * k, 1),
        roll(v, -k, 1),
        roll(v, k, 1),
    )


def weighted(coefs, v, k):
    terms = [m3(a, n) for a, n in zip(coefs, neighbours(v, k))]
    return (terms[0] + terms[1]) + (terms[2] + terms[3]) + (terms[4] + terms[5])


def pair_sum(v):
    rows, lanes = iota(v.shape, 0), iota(v.shape, 1)
    v = v + jnp.where(rows % 2 == 0, roll(v, -1, 0), roll(v, 1, 0))
    v = v + jnp.where(lanes % 32 < 16, roll(v, -16, 1), roll(v, 16, 1))
    return v + jnp.where(lanes % 2 == 0, roll(v, -1, 1), roll(v, 1, 1))


def edge_weights(s, k, scale):
    rows, lanes = iota(s.shape, 0), iota(s.shape, 1)
    coordinate = (rows, lanes // 16, lanes % 16)
    shifts = ((k, 0), (16 * k, 1), (k, 1))
    weights = []
    for where, (step, axis) in zip(coordinate, shifts):
        up = jnp.where(where < 16 - k, scale * (s + roll(s, -step, axis)), 0.0)
        low = jnp.where(where >= k, scale * (s + roll(s, step, axis)), 0.0)
        weights += [up, low]
    return weights, sum(weights[1:], weights[0])


def place(own, low):
    lane = iota((16, 128), 1)
    row = iota((16, 128), 0)
    inner = lane % 16
    parts = []
    for c in range(3):
        halves = []
        for h in range(2):
            r = 3 * h + c
            t = jnp.where(row == 15, own[r : r + 1, :], 0.0)
            t = t - jnp.where(row == 0, low[r : r + 1, :], 0.0)
            if h == 1:
                t = t + jnp.where(lane >= 112, roll(own[8:24], -16 - 16 * c, 1), 0.0)
            else:
                t = t - jnp.where(lane < 16, roll(low[8:24], -16 * c, 1), 0.0)
            t = t + jnp.where(inner == 15, roll(own[24:40], 15 - c - 3 * h, 1), 0.0)
            t = t - jnp.where(inner == 0, roll(low[24:40], -c - 3 * h, 1), 0.0)
            halves.append(t)
        parts.append(jnp.concatenate(halves, axis=1))
    return jnp.concatenate(parts, axis=0)


def pack(v, buf, high):
    lane = iota((16, 128), 1)
    inner = lane % 16
    at = 15 if high else 0
    y = z = None
    for c in range(3):
        for h in range(2):
            r = 3 * h + c
            part = v[16 * c : 16 * c + 16, 128 * h : 128 * h + 128]
            buf[r : r + 1, :] = part[at : at + 1, :]
            t = roll(jnp.where(inner == at, part, 0.0), c + 3 * h - at, 1)
            z = t if z is None else z + t
        if high:
            part = v[16 * c : 16 * c + 16, 128:256]
            t = roll(jnp.where(lane >= 112, part, 0.0), 16 + 16 * c, 1)
        else:
            part = v[16 * c : 16 * c + 16, 0:128]
            t = roll(jnp.where(lane < 16, part, 0.0), 16 * c, 1)
        y = t if y is None else y + t
    buf[6:8, :] = jnp.zeros((2, 128), F32)
    buf[8:24, :] = y
    buf[24:40, :] = z


def from_rows(rows, buf):
    lane = iota((16, 256), 1)
    row = iota((16, 256), 0)
    m, n = iota((256, 128), 0) % 16, iota((256, 128), 1)
    to_y = jnp.where(m == n % 16, 1.0, 0.0)
    to_z = jnp.where(n == (m % 8) * 16 + 3 * (m // 8), 1.0, 0.0)

    def spread(first):
        return jnp.concatenate(
            [jnp.where(lane // 16 == row, rows[first + c : first + c + 1, :], 0.0) for c in range(3)],
            axis=0,
        )

    y = jnp.dot(spread(3), to_y, precision=HI, preferred_element_type=F32)
    z = jnp.dot(spread(6), to_z, precision=HI, preferred_element_type=F32)
    group = iota((16, 128), 1) // 16
    buf[0:3, :] = rows[0:3, 0:128]
    buf[3:6, :] = rows[0:3, 128:256]
    buf[6:8, :] = jnp.zeros((2, 128), F32)
    buf[8:24, :] = sum(jnp.where(group == c, y[16 * c : 16 * c + 16], 0.0) for c in range(3))
    buf[24:40, :] = sum(roll(z[16 * c : 16 * c + 16], c, 1) for c in range(3))


def to_rows(faces, buf, slot):
    lane = iota((16, 256), 1)
    row = iota((16, 256), 0)
    n, m = iota((128, 256), 0), iota((128, 256), 1) % 16
    from_y = jnp.where(n == m, 1.0, 0.0)
    from_z = jnp.where(n == (m % 8) * 16 + 3 * (m // 8), 1.0, 0.0)
    y = jnp.concatenate([roll(faces[8:24], -16 * c, 1) for c in range(3)], axis=0)
    z = jnp.concatenate([roll(faces[24:40], -c, 1) for c in range(3)], axis=0)
    y = jnp.dot(y, from_y, precision=HI, preferred_element_type=F32)
    z = jnp.dot(z, from_z, precision=HI, preferred_element_type=F32)
    buf[slot, 0:3, 0:128] = faces[0:3]
    buf[slot, 0:3, 128:256] = faces[3:6]
    for c in range(3):
        for first, t in ((3, y), (6, z)):
            t = jnp.where(lane // 16 == row, t[16 * c : 16 * c + 16], 0.0)
            buf[slot, first + c : first + c + 1, :] = jnp.sum(t, axis=0, keepdims=True)


def partial_dot(a, b):
    t = jnp.sum(a * b, axis=0, keepdims=True)
    return t[:, 0:128] + t[:, 128:256]


def invert_columns(columns, row):
    for t in range(0, 8, 2):
        p, q = columns[t][t : t + 1], columns[t][t + 1 : t + 2]
        s = columns[t + 1][t + 1 : t + 2]
        d = 1.0 / p
        e = q * d
        p = 1.0 / (s - q * e)
        q = e * p
        s = d + e * q
        pair = (row == t) | (row == t + 1)
        c0 = jnp.where(pair, jnp.where(row == t, -1.0, 0.0), columns[t])
        c1 = jnp.where(pair, jnp.where(row == t, 0.0, -1.0), columns[t + 1])
        updated = []
        for j in range(8):
            if j == t:
                base, w0, w1 = 0.0, s, -q
            elif j == t + 1:
                base, w0, w1 = 0.0, -q, p
            else:
                a, b = columns[j][t : t + 1], columns[j][t + 1 : t + 2]
                base = jnp.where(pair, 0.0, columns[j])
                w0, w1 = s * a - q * b, p * b - q * a
            updated.append(base - c0 * w0 - c1 * w1)
        columns = updated
    return columns


def eliminate(matrix):
    count = matrix.shape[0] // 8
    row, lane = iota((8, 128), 0), iota((8, 128), 1)
    rows = [matrix[8 * i : 8 * i + 8, :] for i in range(count)]
    for k in range(count):
        pivot = rows[k]
        first = 8 * k
        columns = [
            jnp.broadcast_to(pivot[:, first + t : first + t + 1], (8, 128)) for t in range(8)
        ]
        inverse = invert_columns(columns, row)
        scaled = inverse[0] * pivot[0:1]
        for t in range(1, 8):
            scaled = scaled + inverse[t] * pivot[t : t + 1]
        for t in range(8):
            scaled = jnp.where(lane == first + t, inverse[t], scaled)
        hit = (lane >= first) & (lane < first + 8)
        for i in [(k + 1 + i) % count for i in range(count - 1)]:
            change = None
            for t in range(0, 8, 2):
                c0 = rows[i][:, first + t : first + t + 1]
                c1 = rows[i][:, first + t + 1 : first + t + 2]
                term = c0 * scaled[t : t + 1] + c1 * scaled[t + 1 : t + 2]
                change = term if change is None else change + term
            rows[i] = jnp.where(hit, 0.0, rows[i]) - change
        rows[k] = scaled
    for i in range(count):
        matrix[8 * i : 8 * i + 8, :] = rows[i]


def kernel(
    G, Y, Z, mult_hbm, res_hbm, class_hbm, moduli_ref, panel_hbm, lam_ref, out_ref,
    mult_ref, res_ref, class_ref, panel_ref, matrix, panel, sent_hi, sent_lo, got_hi,
    got_lo, corner_out, corner_in, tiles, x_in, yc_in, z_in, rows, load_sem, send_sem,
    recv_sem, far_sem,
):
    loads = [
        pltpu.make_async_copy(src, dst, load_sem.at[i])
        for i, (src, dst) in enumerate(
            (
                (res_hbm, res_ref),
                (panel_hbm, panel_ref),
                (class_hbm, class_ref),
                (mult_hbm, mult_ref),
            )
        )
    ]
    for load in loads:
        load.start()

    sub, member = lax.axis_index("sub"), lax.axis_index("grp")
    n_sub = Y * Z * 2
    grid_row, grid_col = sub // SPAN, sub % SPAN
    upper = (
        ((sub + SPAN) % n_sub, member),
        (grid_row * SPAN + (grid_col + 1) % SPAN, member),
        (sub, (member + 1) % G),
    )
    lower = (
        ((sub + n_sub - SPAN) % n_sub, member),
        (grid_row * SPAN + (grid_col + SPAN - 1) % SPAN, member),
        (sub, (member + G - 1) % G),
    )
    upper_ok = [
        (grid_row < n_sub // SPAN - 1).astype(F32),
        (grid_col < SPAN - 1).astype(F32),
        (member < G - 1).astype(F32),
    ]
    lower_ok = [
        (grid_row > 0).astype(F32),
        (grid_col > 0).astype(F32),
        (member > 0).astype(F32),
    ]
    core, z, y = sub % 2, (sub // 2) % Z, sub // (2 * Z)
    by_distance = lambda n: sorted(range(1, n), key=lambda i: -min(i, n - i))
    x_partners = [(sub, (member + i) % G) for i in by_distance(G)]
    yc_partners = [
        (((y + i) % Y * Z + z) * 2 + (core + c) % 2, member)
        for i in by_distance(Y) + [0]
        for c in (1, 0)
        if (i, c) != (0, 0)
    ]
    along_z = lambda i: ((y * Z + (z + i) % Z) * 2 + core, member)
    z_partners = [along_z(i) for i in by_distance(Z)]

    barrier = pltpu.get_barrier_semaphore()
    greeted = [upper[0], lower[0], upper[1], lower[1]] + x_partners
    greeted += [p for p in yc_partners if p is not yc_partners[-1]]
    reach = min(2, Z // 2)
    greeted += [along_z(i) for n in range(1, reach + 1) for i in (n, Z - n)]
    for device in greeted:
        pl.semaphore_signal(barrier, inc=1, device_id=device, device_id_type=MESH)

    copies = []

    def send(src, dst, device):
        i = len(copies)
        copy = pltpu.make_async_remote_copy(
            src_ref=src, dst_ref=dst, send_sem=send_sem.at[i], recv_sem=recv_sem.at[i],
            device_id=device, device_id_type=MESH,
        )
        copy.start()
        copies.append(copy)
        return copy

    def wait(group):
        for copy in group:
            copy.wait_recv()

    spans = ((0, 8), (8, 24), (24, 40))
    order = (0, 2, 1)

    def exchange(e, both=True, up=True):
        group = []
        for k in order:
            first, last = spans[k]
            if up:
                group.append(
                    send(sent_hi.at[e, first:last], got_hi.at[e, first:last], upper[k])
                )
            if both:
                group.append(
                    send(sent_lo.at[e, first:last], got_lo.at[e, first:last], lower[k])
                )
        return group

    face_row = iota((40, 128), 0)

    def face_mask(ok):
        return jnp.where(face_row < 8, ok[0], jnp.where(face_row < 24, ok[1], ok[2]))

    up_mask, low_mask = face_mask(upper_ok), face_mask(lower_ok)
    row9 = iota((9, 256), 0)
    row_mask = jnp.where(
        row9 < 3, upper_ok[0], jnp.where(row9 < 6, upper_ok[1], upper_ok[2])
    )

    size = G * CORNER
    own_rows = pl.ds(pl.multiple_of(member * CORNER, 8), CORNER)
    panel[...] = jnp.zeros((CORNER, 128), F32)
    loads[1].wait()
    panel[:, 0:size] = panel_ref[0]
    matrix[own_rows, :] = panel[...]

    loads[0].wait()
    residual = res_ref[0] * row_mask
    from_rows(residual, sent_hi.at[0])
    rows[0] = residual

    loads[2].wait()
    classes = class_ref[0]
    stiffness = jnp.zeros((16, 256), F32)
    for level in range(8):
        stiffness = stiffness + jnp.where(classes == level, moduli_ref[level], 0.0)
    weight, total = edge_weights(stiffness, 1, 0.5)
    diagonal = 0.5 * stiffness + total
    scale = DAMP / diagonal
    relax = [scale * w for w in weight]
    block_mean = pair_sum(stiffness) * 0.125
    coarse_weight, coarse_total = edge_weights(block_mean, 2, 2.0)
    coarse_scale = DAMP / (4.0 * block_mean + coarse_total)
    coarse_relax = [coarse_scale * w for w in coarse_weight]

    def operator(v):
        return m3(diagonal, v) - weighted(weight, v, 1)

    def vcycle(f):
        g = m3(scale, f)
        v = g
        v = (1.0 - DAMP) * v + g + weighted(relax, v, 1)
        h = m3(coarse_scale, pair_sum(f - operator(v)))
        e = h
        for _ in range(3):
            e = (1.0 - DAMP) * e + h + weighted(coarse_relax, e, 2)
        v = v + e
        for _ in range(2):
            v = (1.0 - DAMP) * v + g + weighted(relax, v, 1)
        return v

    lanes = iota((1, 256), 1)
    ramp_y = (lanes // 16).astype(F32) / 15.0
    ramp_z = (lanes % 16).astype(F32) / 15.0
    plane = [
        by * bz for by in (1.0 - ramp_y, ramp_y) for bz in (1.0 - ramp_z, ramp_z)
    ]
    ramp_x = iota((16, 256), 0).astype(F32) / 15.0
    row8, lane8 = iota((8, 128), 0), iota((8, 128), 1)
    row8w = iota((8, 256), 0)
    plane8 = sum(jnp.where(row8w % 4 == n, plane[n], 0.0) for n in range(4))

    def corner_sums(f):
        t = jnp.zeros((8, 256), F32)
        for c in range(3):
            part = f[16 * c : 16 * c + 16]
            for a, ramp in ((0, 1.0 - ramp_x), (1, ramp_x)):
                line = jnp.sum(part * ramp, axis=0, keepdims=True)
                t = t + jnp.where(row8w == 2 * c + a, line, 0.0)
        result = jnp.zeros((8, 128), F32)
        for n in range(4):
            s = t * plane[n]
            s = jnp.sum(s[:, 0:128] + s[:, 128:256], axis=1, keepdims=True)
            at = (lane8 == member * CORNER + row8 * 4 + n) & (row8 < 6)
            result = result + jnp.where(at, s, 0.0)
        return result

    def corner_send(e, f):
        corner_out[e] = corner_sums(f)
        return [
            send(corner_out.at[e], corner_in.at[e, i], device)
            for i, device in enumerate(x_partners)
        ]

    def corner_rhs(e):
        rhs = corner_out[e]
        for i in range(G - 1):
            rhs = rhs + corner_in[e, i]
        return jnp.sum(rhs, axis=0, keepdims=True)

    row_m, lane_m = iota((size, 128), 0), iota((size, 128), 1)

    def as_column(line):
        return jnp.sum(jnp.where(row_m == lane_m, line, 0.0), axis=1, keepdims=True)

    def corner_field(rhs):
        solved = jnp.sum(matrix[own_rows, :] * rhs, axis=1, keepdims=True)
        parts = []
        for c in range(3):
            t = solved[8 * c : 8 * c + 8] * plane8
            t0 = jnp.sum(jnp.where(row8w < 4, t, 0.0), axis=0, keepdims=True)
            t1 = jnp.sum(jnp.where(row8w >= 4, t, 0.0), axis=0, keepdims=True)
            parts.append((1.0 - ramp_x) * t0 + ramp_x * t1)
        return jnp.concatenate(parts, axis=0)

    def far_signal(distance, slot):
        for i in (distance, Z - distance):
            pl.semaphore_signal(
                far_sem.at[slot], inc=1, device_id=along_z(i), device_id_type=MESH
            )

    pl.semaphore_wait(barrier, len(greeted))

    group = exchange(0, both=False)
    panels = [send(panel, matrix.at[own_rows, :], device) for device in x_partners]
    if Z > 4:
        far_signal(2, 0)
    wait(group)
    f_r = place(sent_hi[0], got_hi[0] * low_mask)

    image = operator(f_r)
    pack(image, sent_hi.at[1], True)
    pack(image, sent_lo.at[1], False)
    group = exchange(1)
    dots = [0.25 * partial_dot(f_r, image)]
    if Z > 4:
        pl.semaphore_wait(far_sem.at[0], 2)
        if Z > 8:
            far_signal(4, 1)
    wait(panels)
    eliminate(matrix)
    wait(group)
    u = (sent_hi[1] - got_lo[1]) * (0.25 * up_mask)
    f_u = place(u, (got_hi[1] - sent_lo[1]) * (0.25 * low_mask))

    group = corner_send(0, f_u)
    v = vcycle(f_u)
    wait(group)
    rhs_u = corner_rhs(0)
    v = v + corner_field(rhs_u)
    pack(v, sent_hi.at[2], True)
    pack(v, sent_lo.at[2], False)
    group = exchange(2)
    dots.append(partial_dot(f_u, v))
    column_u = as_column(rhs_u)
    to_rows(u, rows, 1)
    wait(group)
    q = (sent_hi[2] - got_lo[2]) * up_mask
    f_q = place(q, (got_hi[2] - sent_lo[2]) * low_mask)

    image = operator(f_q)
    pack(image, sent_hi.at[3], True)
    pack(image, sent_lo.at[3], False)
    group = exchange(3)
    dots.append(0.25 * partial_dot(f_r, image))
    dots.append(0.25 * partial_dot(f_q, image))
    if Z > 8:
        pl.semaphore_wait(far_sem.at[1], 2)
    to_rows(q, rows, 2)
    wait(group)
    w = (sent_hi[3] - got_lo[3]) * (0.25 * up_mask)
    f_w = place(w, (got_hi[3] - sent_lo[3]) * (0.25 * low_mask))

    def spread(slot, tile, landing, partners):
        tiles[slot] = tile
        return [
            send(tiles.at[slot], landing.at[i], device) for i, device in enumerate(partners)
        ]

    def collect(group, tile, landing):
        wait(group)
        for i in range(landing.shape[0]):
            tile = tile + landing[i]
        return tile

    corners = corner_send(1, f_w)
    v = vcycle(f_w)
    dots.append(partial_dot(f_u, v))
    dots.append(partial_dot(f_w, v))
    tile = jnp.zeros((8, 128), F32)
    for i, d in enumerate(dots):
        tile = tile + jnp.where(row8 == i, d, 0.0)
    group = spread(0, tile, x_in, x_partners)
    wait(corners)
    rhs_w = corner_rhs(1)
    solved_w = jnp.sum(matrix[...] * rhs_w, axis=1, keepdims=True)
    coarse_us = jnp.sum(column_u * solved_w, axis=0, keepdims=True)
    coarse_ws = jnp.sum(as_column(rhs_w) * solved_w, axis=0, keepdims=True)
    coarse = jnp.where(row8 == 4, coarse_us, jnp.where(row8 == 5, coarse_ws, 0.0))
    tile = tile + jnp.where(lane8 == 0, coarse, 0.0)
    tile = collect(group, tile, x_in)
    group = spread(1, tile, yc_in, yc_partners)
    v = v + corner_field(rhs_w)
    pack(v, sent_hi.at[4], True)
    pack(v, sent_lo.at[4], False)
    last = exchange(4, up=False)
    to_rows(w, rows, 3)
    tile = collect(group, tile, yc_in)
    group = spread(2, tile, z_in, z_partners)
    wait(last)
    to_rows((sent_hi[4] - got_lo[4]) * up_mask, rows, 4)
    loads[3].wait()
    for copy in copies:
        copy.wait_send()
    tile = collect(group, tile, z_in)

    sums = jnp.sum(tile, axis=1, keepdims=True)
    ru, uq, rw, qw, us, ws = [sums[i : i + 1, :] for i in range(6)]
    a = ru / uq
    next_inner = ru - a * (rw + uq) + a * a * qw
    c = 1.0 + next_inner / ru
    curve = c * c * uq - c * a * (us + qw) + a * a * ws
    b = next_inner / curve
    first, second = a + b * c, a * b
    lam_ref[0] = mult_ref[0] * row_mask + first * rows[1] - second * rows[3]
    out_ref[0] = rows[0] - first * rows[2] + second * rows[4]


def solution(mesh):
    G, n_sub = mesh.shape["grp"], mesh.shape["sub"]
    Z = min(16, n_sub // 2)
    Y = n_sub // (2 * Z)
    size = G * CORNER
    copies = 3 + 3 * 6 + 3 + 4 * (G - 1) + (2 * Y - 1) + (Z - 1)

    def per_device(multipliers, residual, stiff_class, moduli, coarse_panel):
        vmem = pl.BlockSpec(memory_space=pltpu.VMEM)
        hbm = pl.BlockSpec(memory_space=pl.ANY)
        return pl.pallas_call(
            functools.partial(kernel, G, Y, Z),
            out_shape=[jax.ShapeDtypeStruct((1, 9, 256), F32)] * 2,
            in_specs=[hbm, hbm, hbm, pl.BlockSpec(memory_space=pltpu.SMEM), hbm],
            out_specs=[vmem, vmem],
            scratch_shapes=[
                pltpu.VMEM((1, 9, 256), F32),
                pltpu.VMEM((1, 9, 256), F32),
                pltpu.VMEM((1, 16, 256), jnp.int32),
                pltpu.VMEM((1, CORNER, size), F32),
                pltpu.VMEM((size, 128), F32),
                pltpu.VMEM((CORNER, 128), F32),
                pltpu.VMEM((5, 40, 128), F32),
                pltpu.VMEM((5, 40, 128), F32),
                pltpu.VMEM((5, 40, 128), F32),
                pltpu.VMEM((5, 40, 128), F32),
                pltpu.VMEM((2, 8, 128), F32),
                pltpu.VMEM((2, G - 1, 8, 128), F32),
                pltpu.VMEM((3, 8, 128), F32),
                pltpu.VMEM((G - 1, 8, 128), F32),
                pltpu.VMEM((2 * Y - 1, 8, 128), F32),
                pltpu.VMEM((Z - 1, 8, 128), F32),
                pltpu.VMEM((5, 9, 256), F32),
                pltpu.SemaphoreType.DMA((4,)),
                pltpu.SemaphoreType.DMA((copies,)),
                pltpu.SemaphoreType.DMA((copies,)),
                pltpu.SemaphoreType.REGULAR((2,)),
            ],
            compiler_params=pltpu.CompilerParams(
                collective_id=0, has_side_effects=True, vmem_limit_bytes=32 * 1024 * 1024
            ),
            name="feti",
        )(multipliers, residual, stiff_class, moduli, coarse_panel)

    device = P(("sub", "grp"), None, None)
    return jax.shard_map(
        per_device,
        mesh=mesh,
        in_specs=(device, device, device, P(), device),
        out_specs=(device, device),
        check_vma=False,
    )
```

```python
import functools

import jax
import jax.numpy as jnp
from jax import lax
from jax.experimental import pallas as pl
from jax.experimental.pallas import tpu as pltpu
from jax.sharding import PartitionSpec as P

MESH = pl.DeviceIdType.MESH
F32 = jnp.float32
SPAN = 4
CORNER = 24
DAMP = 0.8
HI = lax.Precision.HIGHEST


def roll(x, shift, axis):
    shift = shift % x.shape[axis]
    return x if shift == 0 else pltpu.roll(x, shift, axis)


def iota(shape, axis):
    return lax.broadcasted_iota(jnp.int32, shape, axis)


def m3(coef, field):
    return (field.reshape(3, 16, 256) * coef[None]).reshape(48, 256)


def neighbours(v, k):
    return (
        roll(v, -k, 0),
        roll(v, k, 0),
        roll(v, -16 * k, 1),
        roll(v, 16 * k, 1),
        roll(v, -k, 1),
        roll(v, k, 1),
    )


def weighted(coefs, v, k):
    terms = [m3(a, n) for a, n in zip(coefs, neighbours(v, k))]
    return (terms[0] + terms[1]) + (terms[2] + terms[3]) + (terms[4] + terms[5])


def pair_sum(v):
    rows, lanes = iota(v.shape, 0), iota(v.shape, 1)
    v = v + jnp.where(rows % 2 == 0, roll(v, -1, 0), roll(v, 1, 0))
    v = v + jnp.where(lanes % 32 < 16, roll(v, -16, 1), roll(v, 16, 1))
    return v + jnp.where(lanes % 2 == 0, roll(v, -1, 1), roll(v, 1, 1))


def edge_weights(s, k, scale):
    rows, lanes = iota(s.shape, 0), iota(s.shape, 1)
    coordinate = (rows, lanes // 16, lanes % 16)
    shifts = ((k, 0), (16 * k, 1), (k, 1))
    weights = []
    for where, (step, axis) in zip(coordinate, shifts):
        up = jnp.where(where < 16 - k, scale * (s + roll(s, -step, axis)), 0.0)
        low = jnp.where(where >= k, scale * (s + roll(s, step, axis)), 0.0)
        weights += [up, low]
    return weights, sum(weights[1:], weights[0])


def place(own, low):
    lane = iota((16, 128), 1)
    row = iota((16, 128), 0)
    inner = lane % 16
    parts = []
    for c in range(3):
        halves = []
        for h in range(2):
            r = 3 * h + c
            t = jnp.where(row == 15, own[r : r + 1, :], 0.0)
            t = t - jnp.where(row == 0, low[r : r + 1, :], 0.0)
            if h == 1:
                t = t + jnp.where(lane >= 112, roll(own[8:24], -16 - 16 * c, 1), 0.0)
            else:
                t = t - jnp.where(lane < 16, roll(low[8:24], -16 * c, 1), 0.0)
            t = t + jnp.where(inner == 15, roll(own[24:40], 15 - c - 3 * h, 1), 0.0)
            t = t - jnp.where(inner == 0, roll(low[24:40], -c - 3 * h, 1), 0.0)
            halves.append(t)
        parts.append(jnp.concatenate(halves, axis=1))
    return jnp.concatenate(parts, axis=0)


def pack(v, buf, high):
    lane = iota((16, 128), 1)
    inner = lane % 16
    at = 15 if high else 0
    y = z = None
    for c in range(3):
        for h in range(2):
            r = 3 * h + c
            part = v[16 * c : 16 * c + 16, 128 * h : 128 * h + 128]
            buf[r : r + 1, :] = part[at : at + 1, :]
            t = roll(jnp.where(inner == at, part, 0.0), c + 3 * h - at, 1)
            z = t if z is None else z + t
        if high:
            part = v[16 * c : 16 * c + 16, 128:256]
            t = roll(jnp.where(lane >= 112, part, 0.0), 16 + 16 * c, 1)
        else:
            part = v[16 * c : 16 * c + 16, 0:128]
            t = roll(jnp.where(lane < 16, part, 0.0), 16 * c, 1)
        y = t if y is None else y + t
    buf[6:8, :] = jnp.zeros((2, 128), F32)
    buf[8:24, :] = y
    buf[24:40, :] = z


def from_rows(rows, buf):
    lane = iota((16, 256), 1)
    row = iota((16, 256), 0)
    m, n = iota((256, 128), 0) % 16, iota((256, 128), 1)
    to_y = jnp.where(m == n % 16, 1.0, 0.0)
    to_z = jnp.where(n == (m % 8) * 16 + 3 * (m // 8), 1.0, 0.0)

    def spread(first):
        return jnp.concatenate(
            [jnp.where(lane // 16 == row, rows[first + c : first + c + 1, :], 0.0) for c in range(3)],
            axis=0,
        )

    y = jnp.dot(spread(3), to_y, precision=HI, preferred_element_type=F32)
    z = jnp.dot(spread(6), to_z, precision=HI, preferred_element_type=F32)
    group = iota((16, 128), 1) // 16
    buf[0:3, :] = rows[0:3, 0:128]
    buf[3:6, :] = rows[0:3, 128:256]
    buf[6:8, :] = jnp.zeros((2, 128), F32)
    buf[8:24, :] = sum(jnp.where(group == c, y[16 * c : 16 * c + 16], 0.0) for c in range(3))
    buf[24:40, :] = sum(roll(z[16 * c : 16 * c + 16], c, 1) for c in range(3))


def to_rows(faces, buf, slot):
    lane = iota((16, 256), 1)
    row = iota((16, 256), 0)
    n, m = iota((128, 256), 0), iota((128, 256), 1) % 16
    from_y = jnp.where(n == m, 1.0, 0.0)
    from_z = jnp.where(n == (m % 8) * 16 + 3 * (m // 8), 1.0, 0.0)
    y = jnp.concatenate([roll(faces[8:24], -16 * c, 1) for c in range(3)], axis=0)
    z = jnp.concatenate([roll(faces[24:40], -c, 1) for c in range(3)], axis=0)
    y = jnp.dot(y, from_y, precision=HI, preferred_element_type=F32)
    z = jnp.dot(z, from_z, precision=HI, preferred_element_type=F32)
    buf[slot, 0:3, 0:128] = faces[0:3]
    buf[slot, 0:3, 128:256] = faces[3:6]
    for c in range(3):
        for first, t in ((3, y), (6, z)):
            t = jnp.where(lane // 16 == row, t[16 * c : 16 * c + 16], 0.0)
            buf[slot, first + c : first + c + 1, :] = jnp.sum(t, axis=0, keepdims=True)


def partial_dot(a, b):
    t = jnp.sum(a * b, axis=0, keepdims=True)
    return t[:, 0:128] + t[:, 128:256]


def invert_columns(columns, row):
    for t in range(0, 8, 2):
        p, q = columns[t][t : t + 1], columns[t][t + 1 : t + 2]
        s = columns[t + 1][t + 1 : t + 2]
        d = 1.0 / p
        e = q * d
        p = 1.0 / (s - q * e)
        q = e * p
        s = d + e * q
        pair = (row == t) | (row == t + 1)
        c0 = jnp.where(pair, jnp.where(row == t, -1.0, 0.0), columns[t])
        c1 = jnp.where(pair, jnp.where(row == t, 0.0, -1.0), columns[t + 1])
        updated = []
        for j in range(8):
            if j == t:
                base, w0, w1 = 0.0, s, -q
            elif j == t + 1:
                base, w0, w1 = 0.0, -q, p
            else:
                a, b = columns[j][t : t + 1], columns[j][t + 1 : t + 2]
                base = jnp.where(pair, 0.0, columns[j])
                w0, w1 = s * a - q * b, p * b - q * a
            updated.append(base - c0 * w0 - c1 * w1)
        columns = updated
    return columns


def eliminate(matrix):
    count = matrix.shape[0] // 8
    row, lane = iota((8, 128), 0), iota((8, 128), 1)
    rows = [matrix[8 * i : 8 * i + 8, :] for i in range(count)]
    for k in range(count):
        pivot = rows[k]
        first = 8 * k
        columns = [
            jnp.broadcast_to(pivot[:, first + t : first + t + 1], (8, 128)) for t in range(8)
        ]
        inverse = invert_columns(columns, row)
        scaled = inverse[0] * pivot[0:1]
        for t in range(1, 8):
            scaled = scaled + inverse[t] * pivot[t : t + 1]
        for t in range(8):
            scaled = jnp.where(lane == first + t, inverse[t], scaled)
        hit = (lane >= first) & (lane < first + 8)
        for i in [(k + 1 + i) % count for i in range(count - 1)]:
            change = None
            for t in range(0, 8, 2):
                c0 = rows[i][:, first + t : first + t + 1]
                c1 = rows[i][:, first + t + 1 : first + t + 2]
                term = c0 * scaled[t : t + 1] + c1 * scaled[t + 1 : t + 2]
                change = term if change is None else change + term
            rows[i] = jnp.where(hit, 0.0, rows[i]) - change
        rows[k] = scaled
    for i in range(count):
        matrix[8 * i : 8 * i + 8, :] = rows[i]


def kernel(
    G, Y, Z, mult_hbm, res_hbm, class_hbm, moduli_hbm, panel_hbm, lam_ref, out_ref,
    mult_ref, res_ref, class_ref, moduli_ref, panel_ref, matrix, panel, sent_hi, sent_lo, got_hi,
    got_lo, corner_out, corner_in, tiles, x_in, yc_in, z_in, rows, load_sem, send_sem,
    recv_sem, far_sem,
):
    loads = [
        pltpu.make_async_copy(src, dst, load_sem.at[i])
        for i, (src, dst) in enumerate(
            (
                (res_hbm, res_ref),
                (panel_hbm, panel_ref),
                (class_hbm, class_ref),
                (mult_hbm, mult_ref),
                (moduli_hbm, moduli_ref),
            )
        )
    ]
    loads[0].start()

    sub, member = lax.axis_index("sub"), lax.axis_index("grp")
    n_sub = Y * Z * 2
    grid_row, grid_col = sub // SPAN, sub % SPAN
    upper = (
        ((sub + SPAN) % n_sub, member),
        (grid_row * SPAN + (grid_col + 1) % SPAN, member),
        (sub, (member + 1) % G),
    )
    lower = (
        ((sub + n_sub - SPAN) % n_sub, member),
        (grid_row * SPAN + (grid_col + SPAN - 1) % SPAN, member),
        (sub, (member + G - 1) % G),
    )
    upper_ok = [
        (grid_row < n_sub // SPAN - 1).astype(F32),
        (grid_col < SPAN - 1).astype(F32),
        (member < G - 1).astype(F32),
    ]
    lower_ok = [
        (grid_row > 0).astype(F32),
        (grid_col > 0).astype(F32),
        (member > 0).astype(F32),
    ]
    core, z, y = sub % 2, (sub // 2) % Z, sub // (2 * Z)
    by_distance = lambda n: sorted(range(1, n), key=lambda i: -min(i, n - i))
    x_partners = [(sub, (member + i) % G) for i in by_distance(G)]
    yc_partners = [
        (((y + i) % Y * Z + z) * 2 + (core + c) % 2, member)
        for i in by_distance(Y) + [0]
        for c in (1, 0)
        if (i, c) != (0, 0)
    ]
    along_z = lambda i: ((y * Z + (z + i) % Z) * 2 + core, member)
    z_partners = [along_z(i) for i in by_distance(Z)]

    barrier = pltpu.get_barrier_semaphore()
    greeted = [upper[0], lower[0], upper[1], lower[1]] + x_partners
    greeted += [p for p in yc_partners if p is not yc_partners[-1]]
    reach = min(2, Z // 2)
    greeted += [along_z(i) for n in range(1, reach + 1) for i in (n, Z - n)]
    for device in greeted:
        pl.semaphore_signal(barrier, inc=1, device_id=device, device_id_type=MESH)

    for load in loads[1:]:
        load.start()

    copies = []

    def send(src, dst, device):
        i = len(copies)
        copy = pltpu.make_async_remote_copy(
            src_ref=src, dst_ref=dst, send_sem=send_sem.at[i], recv_sem=recv_sem.at[i],
            device_id=device, device_id_type=MESH,
        )
        copy.start()
        copies.append(copy)
        return copy

    def wait(group):
        for copy in group:
            copy.wait_recv()

    spans = ((0, 8), (8, 24), (24, 40))
    order = (0, 2, 1)

    def exchange(e, both=True, up=True):
        group = []
        for k in order:
            first, last = spans[k]
            if up:
                group.append(
                    send(sent_hi.at[e, first:last], got_hi.at[e, first:last], upper[k])
                )
            if both:
                group.append(
                    send(sent_lo.at[e, first:last], got_lo.at[e, first:last], lower[k])
                )
        return group

    face_row = iota((40, 128), 0)

    def face_mask(ok):
        return jnp.where(face_row < 8, ok[0], jnp.where(face_row < 24, ok[1], ok[2]))

    up_mask, low_mask = face_mask(upper_ok), face_mask(lower_ok)
    row9 = iota((9, 256), 0)
    row_mask = jnp.where(
        row9 < 3, upper_ok[0], jnp.where(row9 < 6, upper_ok[1], upper_ok[2])
    )

    size = G * CORNER
    own_rows = pl.ds(pl.multiple_of(member * CORNER, 8), CORNER)
    panel[...] = jnp.zeros((CORNER, 128), F32)
    loads[1].wait()
    panel[:, 0:size] = panel_ref[0]
    matrix[own_rows, :] = panel[...]

    loads[0].wait()
    residual = res_ref[:, 0, :] * row_mask
    from_rows(residual, sent_hi.at[0])
    rows[0] = residual

    loads[2].wait()
    loads[4].wait()
    classes = class_ref[0]
    stiffness = jnp.zeros((16, 256), F32)
    for level in range(8):
        stiffness = stiffness + jnp.where(classes == level, moduli_ref[level], 0.0)
    weight, total = edge_weights(stiffness, 1, 0.5)
    diagonal = 0.5 * stiffness + total
    scale = DAMP / diagonal
    relax = [scale * w for w in weight]
    block_mean = pair_sum(stiffness) * 0.125
    coarse_weight, coarse_total = edge_weights(block_mean, 2, 2.0)
    coarse_scale = DAMP / (4.0 * block_mean + coarse_total)
    coarse_relax = [coarse_scale * w for w in coarse_weight]

    def operator(v):
        return m3(diagonal, v) - weighted(weight, v, 1)

    def vcycle(f):
        g = m3(scale, f)
        v = g
        v = (1.0 - DAMP) * v + g + weighted(relax, v, 1)
        h = m3(coarse_scale, pair_sum(f - operator(v)))
        e = h
        for _ in range(3):
            e = (1.0 - DAMP) * e + h + weighted(coarse_relax, e, 2)
        v = v + e
        for _ in range(2):
            v = (1.0 - DAMP) * v + g + weighted(relax, v, 1)
        return v

    lanes = iota((1, 256), 1)
    ramp_y = (lanes // 16).astype(F32) / 15.0
    ramp_z = (lanes % 16).astype(F32) / 15.0
    plane = [
        by * bz for by in (1.0 - ramp_y, ramp_y) for bz in (1.0 - ramp_z, ramp_z)
    ]
    ramp_x = iota((16, 256), 0).astype(F32) / 15.0
    row8, lane8 = iota((8, 128), 0), iota((8, 128), 1)
    row8w = iota((8, 256), 0)
    plane8 = sum(jnp.where(row8w % 4 == n, plane[n], 0.0) for n in range(4))

    def corner_sums(f):
        t = jnp.zeros((8, 256), F32)
        for c in range(3):
            part = f[16 * c : 16 * c + 16]
            for a, ramp in ((0, 1.0 - ramp_x), (1, ramp_x)):
                line = jnp.sum(part * ramp, axis=0, keepdims=True)
                t = t + jnp.where(row8w == 2 * c + a, line, 0.0)
        result = jnp.zeros((8, 128), F32)
        for n in range(4):
            s = t * plane[n]
            s = jnp.sum(s[:, 0:128] + s[:, 128:256], axis=1, keepdims=True)
            at = (lane8 == member * CORNER + row8 * 4 + n) & (row8 < 6)
            result = result + jnp.where(at, s, 0.0)
        return jnp.sum(result, axis=0, keepdims=True)

    def corner_send(e, f):
        corner_out[e] = corner_sums(f)
        return [
            send(corner_out.at[e], corner_in.at[e, i], device)
            for i, device in enumerate(x_partners)
        ]

    def corner_rhs(e):
        rhs = corner_out[e]
        for i in range(G - 1):
            rhs = rhs + corner_in[e, i]
        return rhs

    lane1 = iota((1, 128), 1)

    def summed(products):
        t = jnp.zeros((8, 128), F32)
        for i, d in products:
            t = t + jnp.where(row8 == i, d, 0.0)
        t = jnp.sum(t, axis=1, keepdims=True)
        return jnp.sum(jnp.where(row8 == lane8, t, 0.0), axis=0, keepdims=True)

    row_m, lane_m = iota((size, 128), 0), iota((size, 128), 1)

    def as_column(line):
        return jnp.sum(jnp.where(row_m == lane_m, line, 0.0), axis=1, keepdims=True)

    def corner_field(rhs):
        solved = jnp.sum(matrix[own_rows, :] * rhs, axis=1, keepdims=True)
        parts = []
        for c in range(3):
            t = solved[8 * c : 8 * c + 8] * plane8
            t0 = jnp.sum(jnp.where(row8w < 4, t, 0.0), axis=0, keepdims=True)
            t1 = jnp.sum(jnp.where(row8w >= 4, t, 0.0), axis=0, keepdims=True)
            parts.append((1.0 - ramp_x) * t0 + ramp_x * t1)
        return jnp.concatenate(parts, axis=0)

    def far_signal(distance, slot):
        for i in (distance, Z - distance):
            pl.semaphore_signal(
                far_sem.at[slot], inc=1, device_id=along_z(i), device_id_type=MESH
            )

    pl.semaphore_wait(barrier, len(greeted))

    group = exchange(0, both=False)
    panels = [send(panel, matrix.at[own_rows, :], device) for device in x_partners]
    if Z > 4:
        far_signal(2, 0)
    wait(group)
    f_r = place(sent_hi[0], got_hi[0] * low_mask)

    image = operator(f_r)
    pack(image, sent_hi.at[1], True)
    pack(image, sent_lo.at[1], False)
    group = exchange(1)
    dots = [0.25 * partial_dot(f_r, image)]
    if Z > 4:
        pl.semaphore_wait(far_sem.at[0], 2)
        if Z > 8:
            far_signal(4, 1)
    wait(panels)
    eliminate(matrix)
    wait(group)
    u = (sent_hi[1] - got_lo[1]) * (0.25 * up_mask)
    f_u = place(u, (got_hi[1] - sent_lo[1]) * (0.25 * low_mask))

    group = corner_send(0, f_u)
    v = vcycle(f_u)
    wait(group)
    rhs_u = corner_rhs(0)
    v = v + corner_field(rhs_u)
    pack(v, sent_hi.at[2], True)
    pack(v, sent_lo.at[2], False)
    group = exchange(2)
    dots.append(partial_dot(f_u, v))
    column_u = as_column(rhs_u)
    to_rows(u, rows, 1)
    wait(group)
    q = (sent_hi[2] - got_lo[2]) * up_mask
    f_q = place(q, (got_hi[2] - sent_lo[2]) * low_mask)

    image = operator(f_q)
    pack(image, sent_hi.at[3], True)
    pack(image, sent_lo.at[3], False)
    group = exchange(3)
    dots.append(0.25 * partial_dot(f_r, image))
    dots.append(0.25 * partial_dot(f_q, image))
    if Z > 8:
        pl.semaphore_wait(far_sem.at[1], 2)
    early = summed(list(enumerate(dots)))
    to_rows(q, rows, 2)
    wait(group)
    w = (sent_hi[3] - got_lo[3]) * (0.25 * up_mask)
    f_w = place(w, (got_hi[3] - sent_lo[3]) * (0.25 * low_mask))

    def spread(slot, tile, landing, partners):
        tiles[slot] = tile
        return [
            send(tiles.at[slot], landing.at[i], device) for i, device in enumerate(partners)
        ]

    def collect(group, tile, landing):
        wait(group)
        for i in range(landing.shape[0]):
            tile = tile + landing[i]
        return tile

    corners = corner_send(1, f_w)
    v = vcycle(f_w)
    tile = early + summed([(4, partial_dot(f_u, v)), (5, partial_dot(f_w, v))])
    group = spread(0, tile, x_in, x_partners)
    wait(corners)
    rhs_w = corner_rhs(1)
    solved_w = jnp.sum(matrix[...] * rhs_w, axis=1, keepdims=True)
    coarse_us = jnp.sum(column_u * solved_w, axis=0, keepdims=True)
    coarse_ws = jnp.sum(as_column(rhs_w) * solved_w, axis=0, keepdims=True)
    coarse = jnp.where(lane1 == 4, coarse_us, jnp.where(lane1 == 5, coarse_ws, 0.0))
    tile = tile + coarse
    tile = collect(group, tile, x_in)
    group = spread(1, tile, yc_in, yc_partners)
    v = v + corner_field(rhs_w)
    pack(v, sent_hi.at[4], True)
    pack(v, sent_lo.at[4], False)
    last = exchange(4, up=False)
    to_rows(w, rows, 3)
    tile = collect(group, tile, yc_in)
    group = spread(2, tile, z_in, z_partners)
    wait(last)
    to_rows((sent_hi[4] - got_lo[4]) * up_mask, rows, 4)
    loads[3].wait()
    for copy in copies:
        copy.wait_send()
    tile = collect(group, tile, z_in)

    ru, uq, rw, qw, us, ws = [tile[:, i : i + 1] for i in range(6)]
    a = ru / uq
    next_inner = ru - a * (rw + uq) + a * a * qw
    c = 1.0 + next_inner / ru
    curve = c * c * uq - c * a * (us + qw) + a * a * ws
    b = next_inner / curve
    first, second = a + b * c, a * b
    lam_ref[:, 0, :] = mult_ref[:, 0, :] * row_mask + first * rows[1] - second * rows[3]
    out_ref[:, 0, :] = rows[0] - first * rows[2] + second * rows[4]


def solution(mesh):
    G, n_sub = mesh.shape["grp"], mesh.shape["sub"]
    Z = min(16, n_sub // 2)
    Y = n_sub // (2 * Z)
    size = G * CORNER
    copies = 3 + 3 * 6 + 3 + 4 * (G - 1) + (2 * Y - 1) + (Z - 1)

    def per_device(multipliers, residual, stiff_class, moduli, coarse_panel):
        vmem = pl.BlockSpec(memory_space=pltpu.VMEM)
        hbm = pl.BlockSpec(memory_space=pltpu.HBM)
        face_first = (1, 0, 2)
        in_hbm = lambda x: pltpu.with_memory_space_constraint(x, pltpu.HBM)
        lam, out = pl.pallas_call(
            functools.partial(kernel, G, Y, Z),
            out_shape=[jax.ShapeDtypeStruct((9, 1, 256), F32)] * 2,
            in_specs=[hbm] * 5,
            out_specs=[vmem, vmem],
            scratch_shapes=[
                pltpu.VMEM((9, 1, 256), F32),
                pltpu.VMEM((9, 1, 256), F32),
                pltpu.VMEM((1, 16, 256), jnp.int32),
                pltpu.SMEM((8,), F32),
                pltpu.VMEM((1, CORNER, size), F32),
                pltpu.VMEM((size, 128), F32),
                pltpu.VMEM((CORNER, 128), F32),
                pltpu.VMEM((5, 40, 128), F32),
                pltpu.VMEM((5, 40, 128), F32),
                pltpu.VMEM((5, 40, 128), F32),
                pltpu.VMEM((5, 40, 128), F32),
                pltpu.VMEM((2, 1, 128), F32),
                pltpu.VMEM((2, G - 1, 1, 128), F32),
                pltpu.VMEM((3, 1, 128), F32),
                pltpu.VMEM((G - 1, 1, 128), F32),
                pltpu.VMEM((2 * Y - 1, 1, 128), F32),
                pltpu.VMEM((Z - 1, 1, 128), F32),
                pltpu.VMEM((5, 9, 256), F32),
                pltpu.SemaphoreType.DMA((5,)),
                pltpu.SemaphoreType.DMA((copies,)),
                pltpu.SemaphoreType.DMA((copies,)),
                pltpu.SemaphoreType.REGULAR((2,)),
            ],
            compiler_params=pltpu.CompilerParams(
                collective_id=0, has_side_effects=True, vmem_limit_bytes=32 * 1024 * 1024
            ),
            name="feti",
        )(
            in_hbm(multipliers.transpose(face_first)),
            in_hbm(residual.transpose(face_first)),
            in_hbm(stiff_class),
            in_hbm(moduli),
            in_hbm(coarse_panel),
        )
        return lam.transpose(face_first), out.transpose(face_first)

    device = P(("sub", "grp"), None, None)
    return jax.shard_map(
        per_device,
        mesh=mesh,
        in_specs=(device, device, device, P(), device),
        out_specs=(device, device),
        check_vma=False,
    )
```

```python
import functools

import jax
import jax.numpy as jnp
from jax import lax
from jax.experimental import pallas as pl
from jax.experimental.pallas import tpu as pltpu
from jax.sharding import PartitionSpec as P

MESH = pl.DeviceIdType.MESH
F32 = jnp.float32
SPAN = 4
CORNER = 24
DAMP = 0.8
HI = lax.Precision.HIGHEST


def roll(x, shift, axis):
    shift = shift % x.shape[axis]
    return x if shift == 0 else pltpu.roll(x, shift, axis)


def iota(shape, axis):
    return lax.broadcasted_iota(jnp.int32, shape, axis)


def m3(coef, field):
    return (field.reshape(3, 16, 256) * coef[None]).reshape(48, 256)


def neighbours(v, k):
    return (
        roll(v, -k, 0),
        roll(v, k, 0),
        roll(v, -16 * k, 1),
        roll(v, 16 * k, 1),
        roll(v, -k, 1),
        roll(v, k, 1),
    )


def weighted(coefs, v, k):
    terms = [m3(a, n) for a, n in zip(coefs, neighbours(v, k))]
    return (terms[0] + terms[1]) + (terms[2] + terms[3]) + (terms[4] + terms[5])


def pair_sum(v):
    rows, lanes = iota(v.shape, 0), iota(v.shape, 1)
    v = v + jnp.where(rows % 2 == 0, roll(v, -1, 0), roll(v, 1, 0))
    v = v + jnp.where(lanes % 32 < 16, roll(v, -16, 1), roll(v, 16, 1))
    return v + jnp.where(lanes % 2 == 0, roll(v, -1, 1), roll(v, 1, 1))


def edge_weights(s, k, scale):
    rows, lanes = iota(s.shape, 0), iota(s.shape, 1)
    coordinate = (rows, lanes // 16, lanes % 16)
    shifts = ((k, 0), (16 * k, 1), (k, 1))
    weights = []
    for where, (step, axis) in zip(coordinate, shifts):
        up = jnp.where(where < 16 - k, scale * (s + roll(s, -step, axis)), 0.0)
        low = jnp.where(where >= k, scale * (s + roll(s, step, axis)), 0.0)
        weights += [up, low]
    return weights, sum(weights[1:], weights[0])


def place(own, low):
    lane = iota((16, 128), 1)
    row = iota((16, 128), 0)
    inner = lane % 16
    parts = []
    for c in range(3):
        halves = []
        for h in range(2):
            r = 3 * h + c
            t = jnp.where(row == 15, own[r : r + 1, :], 0.0)
            t = t - jnp.where(row == 0, low[r : r + 1, :], 0.0)
            if h == 1:
                t = t + jnp.where(lane >= 112, roll(own[8:24], -16 - 16 * c, 1), 0.0)
            else:
                t = t - jnp.where(lane < 16, roll(low[8:24], -16 * c, 1), 0.0)
            t = t + jnp.where(inner == 15, roll(own[24:40], 15 - c - 3 * h, 1), 0.0)
            t = t - jnp.where(inner == 0, roll(low[24:40], -c - 3 * h, 1), 0.0)
            halves.append(t)
        parts.append(jnp.concatenate(halves, axis=1))
    return jnp.concatenate(parts, axis=0)


def pack(v, buf, high):
    lane = iota((16, 128), 1)
    inner = lane % 16
    at = 15 if high else 0
    y = z = None
    for c in range(3):
        for h in range(2):
            r = 3 * h + c
            part = v[16 * c : 16 * c + 16, 128 * h : 128 * h + 128]
            buf[r : r + 1, :] = part[at : at + 1, :]
            t = roll(jnp.where(inner == at, part, 0.0), c + 3 * h - at, 1)
            z = t if z is None else z + t
        if high:
            part = v[16 * c : 16 * c + 16, 128:256]
            t = roll(jnp.where(lane >= 112, part, 0.0), 16 + 16 * c, 1)
        else:
            part = v[16 * c : 16 * c + 16, 0:128]
            t = roll(jnp.where(lane < 16, part, 0.0), 16 * c, 1)
        y = t if y is None else y + t
    buf[6:8, :] = jnp.zeros((2, 128), F32)
    buf[8:24, :] = y
    buf[24:40, :] = z


def from_rows(rows, buf):
    lane = iota((16, 256), 1)
    row = iota((16, 256), 0)
    m, n = iota((256, 128), 0) % 16, iota((256, 128), 1)
    to_y = jnp.where(m == n % 16, 1.0, 0.0)
    to_z = jnp.where(n == (m % 8) * 16 + 3 * (m // 8), 1.0, 0.0)

    def spread(first):
        return jnp.concatenate(
            [jnp.where(lane // 16 == row, rows[first + c : first + c + 1, :], 0.0) for c in range(3)],
            axis=0,
        )

    y = jnp.dot(spread(3), to_y, precision=HI, preferred_element_type=F32)
    z = jnp.dot(spread(6), to_z, precision=HI, preferred_element_type=F32)
    group = iota((16, 128), 1) // 16
    buf[0:3, :] = rows[0:3, 0:128]
    buf[3:6, :] = rows[0:3, 128:256]
    buf[6:8, :] = jnp.zeros((2, 128), F32)
    buf[8:24, :] = sum(jnp.where(group == c, y[16 * c : 16 * c + 16], 0.0) for c in range(3))
    buf[24:40, :] = sum(roll(z[16 * c : 16 * c + 16], c, 1) for c in range(3))


def to_rows(faces, buf, slot):
    lane = iota((16, 256), 1)
    row = iota((16, 256), 0)
    n, m = iota((128, 256), 0), iota((128, 256), 1) % 16
    from_y = jnp.where(n == m, 1.0, 0.0)
    from_z = jnp.where(n == (m % 8) * 16 + 3 * (m // 8), 1.0, 0.0)
    y = jnp.concatenate([roll(faces[8:24], -16 * c, 1) for c in range(3)], axis=0)
    z = jnp.concatenate([roll(faces[24:40], -c, 1) for c in range(3)], axis=0)
    y = jnp.dot(y, from_y, precision=HI, preferred_element_type=F32)
    z = jnp.dot(z, from_z, precision=HI, preferred_element_type=F32)
    buf[slot, 0:3, 0:128] = faces[0:3]
    buf[slot, 0:3, 128:256] = faces[3:6]
    for c in range(3):
        for first, t in ((3, y), (6, z)):
            t = jnp.where(lane // 16 == row, t[16 * c : 16 * c + 16], 0.0)
            buf[slot, first + c : first + c + 1, :] = jnp.sum(t, axis=0, keepdims=True)


def partial_dot(a, b):
    t = jnp.sum(a * b, axis=0, keepdims=True)
    return t[:, 0:128] + t[:, 128:256]


def invert_columns(columns, row):
    for t in range(0, 8, 2):
        p, q = columns[t][t : t + 1], columns[t][t + 1 : t + 2]
        s = columns[t + 1][t + 1 : t + 2]
        d = 1.0 / p
        e = q * d
        p = 1.0 / (s - q * e)
        q = e * p
        s = d + e * q
        pair = (row == t) | (row == t + 1)
        c0 = jnp.where(pair, jnp.where(row == t, -1.0, 0.0), columns[t])
        c1 = jnp.where(pair, jnp.where(row == t, 0.0, -1.0), columns[t + 1])
        updated = []
        for j in range(8):
            if j == t:
                base, w0, w1 = 0.0, s, -q
            elif j == t + 1:
                base, w0, w1 = 0.0, -q, p
            else:
                a, b = columns[j][t : t + 1], columns[j][t + 1 : t + 2]
                base = jnp.where(pair, 0.0, columns[j])
                w0, w1 = s * a - q * b, p * b - q * a
            updated.append(base - c0 * w0 - c1 * w1)
        columns = updated
    return columns


def eliminate(matrix):
    count = matrix.shape[0] // 8
    row, lane = iota((8, 128), 0), iota((8, 128), 1)
    rows = [matrix[8 * i : 8 * i + 8, :] for i in range(count)]
    for k in range(count):
        pivot = rows[k]
        first = 8 * k
        columns = [
            jnp.broadcast_to(pivot[:, first + t : first + t + 1], (8, 128)) for t in range(8)
        ]
        inverse = invert_columns(columns, row)
        scaled = inverse[0] * pivot[0:1]
        for t in range(1, 8):
            scaled = scaled + inverse[t] * pivot[t : t + 1]
        for t in range(8):
            scaled = jnp.where(lane == first + t, inverse[t], scaled)
        hit = (lane >= first) & (lane < first + 8)
        for i in [(k + 1 + i) % count for i in range(count - 1)]:
            change = None
            for t in range(0, 8, 2):
                c0 = rows[i][:, first + t : first + t + 1]
                c1 = rows[i][:, first + t + 1 : first + t + 2]
                term = c0 * scaled[t : t + 1] + c1 * scaled[t + 1 : t + 2]
                change = term if change is None else change + term
            rows[i] = jnp.where(hit, 0.0, rows[i]) - change
        rows[k] = scaled
    for i in range(count):
        matrix[8 * i : 8 * i + 8, :] = rows[i]


def kernel(
    G, Y, Z, mult_hbm, res_hbm, class_hbm, moduli_hbm, panel_hbm, lam_ref, out_ref,
    mult_ref, res_ref, class_ref, moduli_ref, panel_ref, matrix, panel, sent_hi, sent_lo, got_hi,
    got_lo, corner_out, corner_in, tiles, x_in, sub_in, rows, load_sem, sum_sem, send_sem,
    recv_sem, far_sem,
):
    loads = [
        pltpu.make_async_copy(src, dst, load_sem.at[i])
        for i, (src, dst) in enumerate(
            (
                (res_hbm, res_ref),
                (panel_hbm, panel_ref),
                (class_hbm, class_ref),
                (mult_hbm, mult_ref),
                (moduli_hbm, moduli_ref),
            )
        )
    ]
    loads[0].start()

    sub, member = lax.axis_index("sub"), lax.axis_index("grp")
    n_sub = Y * Z * 2
    grid_row, grid_col = sub // SPAN, sub % SPAN
    upper = (
        ((sub + SPAN) % n_sub, member),
        (grid_row * SPAN + (grid_col + 1) % SPAN, member),
        (sub, (member + 1) % G),
    )
    lower = (
        ((sub + n_sub - SPAN) % n_sub, member),
        (grid_row * SPAN + (grid_col + SPAN - 1) % SPAN, member),
        (sub, (member + G - 1) % G),
    )
    upper_ok = [
        (grid_row < n_sub // SPAN - 1).astype(F32),
        (grid_col < SPAN - 1).astype(F32),
        (member < G - 1).astype(F32),
    ]
    lower_ok = [
        (grid_row > 0).astype(F32),
        (grid_col > 0).astype(F32),
        (member > 0).astype(F32),
    ]
    core, z, y = sub % 2, (sub // 2) % Z, sub // (2 * Z)
    by_distance = lambda n: sorted(range(1, n), key=lambda i: -min(i, n - i))
    x_partners = [(sub, (member + i) % G) for i in by_distance(G)]
    yc_partners = [
        (((y + i) % Y * Z + z) * 2 + (core + c) % 2, member)
        for i in by_distance(Y) + [0]
        for c in (1, 0)
        if (i, c) != (0, 0)
    ]
    along_z = lambda i: ((y * Z + (z + i) % Z) * 2 + core, member)
    distance = lambda o: min(o[0], Y - o[0]) + min(o[1], Z - o[1])
    offsets = [(i, j, c) for i in range(Y) for j in range(Z) for c in range(2)][1:]
    sub_partners = [
        (((y + i) % Y * Z + (z + j) % Z) * 2 + (core + c) % 2, member)
        for i, j, c in sorted(offsets, key=distance, reverse=True)
    ]

    barrier = pltpu.get_barrier_semaphore()
    greeted = [upper[0], lower[0], upper[1], lower[1]] + x_partners
    greeted += [p for p in yc_partners if p is not yc_partners[-1]]
    reach = min(2, Z // 2)
    greeted += [along_z(i) for n in range(1, reach + 1) for i in (n, Z - n)]
    for device in greeted:
        pl.semaphore_signal(barrier, inc=1, device_id=device, device_id_type=MESH)

    for load in loads[1:]:
        load.start()

    copies = []

    def send(src, dst, device):
        i = len(copies)
        copy = pltpu.make_async_remote_copy(
            src_ref=src, dst_ref=dst, send_sem=send_sem.at[i], recv_sem=recv_sem.at[i],
            device_id=device, device_id_type=MESH,
        )
        copy.start()
        copies.append(copy)
        return copy

    def wait(group):
        for copy in group:
            copy.wait_recv()

    spans = ((0, 8), (8, 24), (24, 40))
    order = (0, 2, 1)

    def exchange(e, both=True, up=True):
        group = []
        for k in order:
            first, last = spans[k]
            if up:
                group.append(
                    send(sent_hi.at[e, first:last], got_hi.at[e, first:last], upper[k])
                )
            if both:
                group.append(
                    send(sent_lo.at[e, first:last], got_lo.at[e, first:last], lower[k])
                )
        return group

    face_row = iota((40, 128), 0)

    def face_mask(ok):
        return jnp.where(face_row < 8, ok[0], jnp.where(face_row < 24, ok[1], ok[2]))

    up_mask, low_mask = face_mask(upper_ok), face_mask(lower_ok)
    row9 = iota((9, 256), 0)
    row_mask = jnp.where(
        row9 < 3, upper_ok[0], jnp.where(row9 < 6, upper_ok[1], upper_ok[2])
    )

    size = G * CORNER
    own_rows = pl.ds(pl.multiple_of(member * CORNER, 8), CORNER)
    panel[...] = jnp.zeros((CORNER, 128), F32)
    loads[1].wait()
    panel[:, 0:size] = panel_ref[0]
    matrix[own_rows, :] = panel[...]

    loads[0].wait()
    residual = res_ref[:, 0, :] * row_mask
    from_rows(residual, sent_hi.at[0])
    rows[0] = residual

    loads[2].wait()
    loads[4].wait()
    classes = class_ref[0]
    stiffness = jnp.zeros((16, 256), F32)
    for level in range(8):
        stiffness = stiffness + jnp.where(classes == level, moduli_ref[level], 0.0)
    weight, total = edge_weights(stiffness, 1, 0.5)
    diagonal = 0.5 * stiffness + total
    scale = DAMP / diagonal
    relax = [scale * w for w in weight]
    block_mean = pair_sum(stiffness) * 0.125
    coarse_weight, coarse_total = edge_weights(block_mean, 2, 2.0)
    coarse_scale = DAMP / (4.0 * block_mean + coarse_total)
    coarse_relax = [coarse_scale * w for w in coarse_weight]

    def operator(v):
        return m3(diagonal, v) - weighted(weight, v, 1)

    def before_correction(f):
        g = m3(scale, f)
        v = (1.0 - DAMP) * g + g + weighted(relax, g, 1)
        defect = f - operator(v)
        h = m3(coarse_scale, pair_sum(defect))
        e = h
        for _ in range(3):
            e = (1.0 - DAMP) * e + h + weighted(coarse_relax, e, 2)
        return v, defect, v + e

    def after_correction(f, v):
        g = m3(scale, f)
        for _ in range(2):
            v = (1.0 - DAMP) * v + g + weighted(relax, v, 1)
        return v

    lanes = iota((1, 256), 1)
    ramp_y = (lanes // 16).astype(F32) / 15.0
    ramp_z = (lanes % 16).astype(F32) / 15.0
    plane = [
        by * bz for by in (1.0 - ramp_y, ramp_y) for bz in (1.0 - ramp_z, ramp_z)
    ]
    ramp_x = iota((16, 256), 0).astype(F32) / 15.0
    row8, lane8 = iota((8, 128), 0), iota((8, 128), 1)
    row8w = iota((8, 256), 0)
    plane8 = sum(jnp.where(row8w % 4 == n, plane[n], 0.0) for n in range(4))

    def corner_sums(f):
        t = jnp.zeros((8, 256), F32)
        for c in range(3):
            part = f[16 * c : 16 * c + 16]
            for a, ramp in ((0, 1.0 - ramp_x), (1, ramp_x)):
                line = jnp.sum(part * ramp, axis=0, keepdims=True)
                t = t + jnp.where(row8w == 2 * c + a, line, 0.0)
        result = jnp.zeros((8, 128), F32)
        for n in range(4):
            s = t * plane[n]
            s = jnp.sum(s[:, 0:128] + s[:, 128:256], axis=1, keepdims=True)
            at = (lane8 == member * CORNER + row8 * 4 + n) & (row8 < 6)
            result = result + jnp.where(at, s, 0.0)
        return jnp.sum(result, axis=0, keepdims=True)

    def corner_send(e, f):
        corner_out[e] = corner_sums(f)
        return [
            send(corner_out.at[e], corner_in.at[e, i], device)
            for i, device in enumerate(x_partners)
        ]

    def corner_rhs(e):
        rhs = corner_out[e]
        for i in range(G - 1):
            rhs = rhs + corner_in[e, i]
        return rhs

    lane1 = iota((1, 128), 1)

    def summed(products):
        t = jnp.zeros((8, 128), F32)
        for i, d in products:
            t = t + jnp.where(row8 == i, d, 0.0)
        t = jnp.sum(t, axis=1, keepdims=True)
        return jnp.sum(jnp.where(row8 == lane8, t, 0.0), axis=0, keepdims=True)

    row_m, lane_m = iota((size, 128), 0), iota((size, 128), 1)

    def as_column(line):
        return jnp.sum(jnp.where(row_m == lane_m, line, 0.0), axis=1, keepdims=True)

    def corner_field(rhs):
        solved = jnp.sum(matrix[own_rows, :] * rhs, axis=1, keepdims=True)
        parts = []
        for c in range(3):
            t = solved[8 * c : 8 * c + 8] * plane8
            t0 = jnp.sum(jnp.where(row8w < 4, t, 0.0), axis=0, keepdims=True)
            t1 = jnp.sum(jnp.where(row8w >= 4, t, 0.0), axis=0, keepdims=True)
            parts.append((1.0 - ramp_x) * t0 + ramp_x * t1)
        return jnp.concatenate(parts, axis=0)

    def far_signal(slot):
        step = min((1, 3, 4)[slot], Z // 2 - 1)
        for i in (step, Z - step):
            pl.semaphore_signal(
                far_sem.at[slot], inc=1, device_id=along_z(i), device_id_type=MESH
            )

    def far_wait(slot):
        pl.semaphore_wait(far_sem.at[slot], 2)

    pl.semaphore_wait(barrier, len(greeted))

    group = exchange(0, both=False)
    panels = [send(panel, matrix.at[own_rows, :], device) for device in x_partners]
    far_signal(0)
    wait(group)
    f_r = place(sent_hi[0], got_hi[0] * low_mask)

    image = operator(f_r)
    pack(image, sent_hi.at[1], True)
    pack(image, sent_lo.at[1], False)
    group = exchange(1)
    dots = [0.25 * partial_dot(f_r, image)]
    far_wait(0)
    far_signal(1)
    wait(panels)
    eliminate(matrix)
    wait(group)
    u = (sent_hi[1] - got_lo[1]) * (0.25 * up_mask)
    f_u = place(u, (got_hi[1] - sent_lo[1]) * (0.25 * low_mask))

    group = corner_send(0, f_u)
    _, defect_u, v = before_correction(f_u)
    v = after_correction(f_u, v)
    wait(group)
    rhs_u = corner_rhs(0)
    v = v + corner_field(rhs_u)
    pack(v, sent_hi.at[2], True)
    pack(v, sent_lo.at[2], False)
    group = exchange(2)
    dots.append(partial_dot(f_u, v))
    far_wait(1)
    far_signal(2)
    column_u = as_column(rhs_u)
    to_rows(u, rows, 1)
    wait(group)
    q = (sent_hi[2] - got_lo[2]) * up_mask
    f_q = place(q, (got_hi[2] - sent_lo[2]) * low_mask)

    image = operator(f_q)
    pack(image, sent_hi.at[3], True)
    pack(image, sent_lo.at[3], False)
    group = exchange(3)
    dots.append(0.25 * partial_dot(f_r, image))
    dots.append(0.25 * partial_dot(f_q, image))
    far_wait(2)
    early = summed(list(enumerate(dots)))
    to_rows(q, rows, 2)
    wait(group)
    w = (sent_hi[3] - got_lo[3]) * (0.25 * up_mask)
    f_w = place(w, (got_hi[3] - sent_lo[3]) * (0.25 * low_mask))

    corners = corner_send(1, f_w)
    before, defect_w, after = before_correction(f_w)
    tile = early + summed(
        [
            (4, partial_dot(f_u, before) + partial_dot(defect_u, after)),
            (5, partial_dot(f_w, before) + partial_dot(defect_w, after)),
        ]
    )
    tiles[0] = tile
    group = [
        send(tiles.at[0], x_in.at[i], device) for i, device in enumerate(x_partners)
    ]
    v = after_correction(f_w, after)
    wait(corners)
    rhs_w = corner_rhs(1)
    v = v + corner_field(rhs_w)
    pack(v, sent_lo.at[4], False)
    last = exchange(4, up=False)
    solved_w = jnp.sum(matrix[...] * rhs_w, axis=1, keepdims=True)
    coarse_us = jnp.sum(column_u * solved_w, axis=0, keepdims=True)
    coarse_ws = jnp.sum(as_column(rhs_w) * solved_w, axis=0, keepdims=True)
    coarse = jnp.where(lane1 == 4, coarse_us, jnp.where(lane1 == 5, coarse_ws, 0.0))
    tile = tile + coarse
    wait(group)
    for i in range(G - 1):
        tile = tile + x_in[i]

    tiles[1] = tile
    for i, device in enumerate(sub_partners):
        pltpu.make_async_remote_copy(
            src_ref=tiles.at[1], dst_ref=sub_in.at[i], send_sem=sum_sem.at[0],
            recv_sem=sum_sem.at[1], device_id=device, device_id_type=MESH,
        ).start()
    arrived = pltpu.make_async_remote_copy(
        src_ref=sub_in, dst_ref=sub_in, send_sem=sum_sem.at[0], recv_sem=sum_sem.at[1],
        device_id=sub_partners[0], device_id_type=MESH,
    )
    pack(v, sent_hi.at[4], True)
    to_rows(w, rows, 3)
    wait(last)
    to_rows((sent_hi[4] - got_lo[4]) * up_mask, rows, 4)
    loads[3].wait()
    for copy in copies:
        copy.wait_send()
    arrived.wait_recv()
    parts = [sub_in[i] for i in range(len(sub_partners))] + [tile]
    while len(parts) > 1:
        parts = [sum(parts[i : i + 2][1:], parts[i]) for i in range(0, len(parts), 2)]
    tile = parts[0]
    arrived.wait_send()

    ru, uq, rw, qw, us, ws = [tile[:, i : i + 1] for i in range(6)]
    a = ru / uq
    next_inner = ru - a * (rw + uq) + a * a * qw
    c = 1.0 + next_inner / ru
    curve = c * c * uq - c * a * (us + qw) + a * a * ws
    b = next_inner / curve
    first, second = a + b * c, a * b
    lam_ref[:, 0, :] = mult_ref[:, 0, :] * row_mask + first * rows[1] - second * rows[3]
    out_ref[:, 0, :] = rows[0] - first * rows[2] + second * rows[4]


def solution(mesh):
    G, n_sub = mesh.shape["grp"], mesh.shape["sub"]
    Z = min(16, n_sub // 2)
    Y = n_sub // (2 * Z)
    size = G * CORNER
    copies = 3 + 3 * 6 + 3 + 4 * (G - 1)

    def per_device(multipliers, residual, stiff_class, moduli, coarse_panel):
        vmem = pl.BlockSpec(memory_space=pltpu.VMEM)
        hbm = pl.BlockSpec(memory_space=pltpu.HBM)
        face_first = (1, 0, 2)
        in_hbm = lambda x: pltpu.with_memory_space_constraint(x, pltpu.HBM)
        lam, out = pl.pallas_call(
            functools.partial(kernel, G, Y, Z),
            out_shape=[jax.ShapeDtypeStruct((9, 1, 256), F32)] * 2,
            in_specs=[hbm] * 5,
            out_specs=[vmem, vmem],
            scratch_shapes=[
                pltpu.VMEM((9, 1, 256), F32),
                pltpu.VMEM((9, 1, 256), F32),
                pltpu.VMEM((1, 16, 256), jnp.int32),
                pltpu.SMEM((8,), F32),
                pltpu.VMEM((1, CORNER, size), F32),
                pltpu.VMEM((size, 128), F32),
                pltpu.VMEM((CORNER, 128), F32),
                pltpu.VMEM((5, 40, 128), F32),
                pltpu.VMEM((5, 40, 128), F32),
                pltpu.VMEM((5, 40, 128), F32),
                pltpu.VMEM((5, 40, 128), F32),
                pltpu.VMEM((2, 1, 128), F32),
                pltpu.VMEM((2, G - 1, 1, 128), F32),
                pltpu.VMEM((2, 1, 128), F32),
                pltpu.VMEM((G - 1, 1, 128), F32),
                pltpu.VMEM((n_sub - 1, 1, 128), F32),
                pltpu.VMEM((5, 9, 256), F32),
                pltpu.SemaphoreType.DMA((5,)),
                pltpu.SemaphoreType.DMA((2,)),
                pltpu.SemaphoreType.DMA((copies,)),
                pltpu.SemaphoreType.DMA((copies,)),
                pltpu.SemaphoreType.REGULAR((3,)),
            ],
            compiler_params=pltpu.CompilerParams(
                collective_id=0, has_side_effects=True, vmem_limit_bytes=32 * 1024 * 1024
            ),
            name="feti",
        )(
            in_hbm(multipliers.transpose(face_first)),
            in_hbm(residual.transpose(face_first)),
            in_hbm(stiff_class),
            in_hbm(moduli),
            in_hbm(coarse_panel),
        )
        return lam.transpose(face_first), out.transpose(face_first)

    device = P(("sub", "grp"), None, None)
    return jax.shard_map(
        per_device,
        mesh=mesh,
        in_specs=(device, device, device, P(), device),
        out_specs=(device, device),
        check_vma=False,
    )
```

```python
import functools

import jax
import jax.numpy as jnp
from jax import lax
from jax.experimental import pallas as pl
from jax.experimental.pallas import tpu as pltpu
from jax.sharding import PartitionSpec as P

MESH = pl.DeviceIdType.MESH
F32 = jnp.float32
SPAN = 4
CORNER = 24
DAMP = 0.8
HI = lax.Precision.HIGHEST


def roll(x, shift, axis):
    shift = shift % x.shape[axis]
    return x if shift == 0 else pltpu.roll(x, shift, axis)


def iota(shape, axis):
    return lax.broadcasted_iota(jnp.int32, shape, axis)


def m3(coef, field):
    return (field.reshape(3, 16, 256) * coef[None]).reshape(48, 256)


def neighbours(v, k):
    return (
        roll(v, -k, 0),
        roll(v, k, 0),
        roll(v, -16 * k, 1),
        roll(v, 16 * k, 1),
        roll(v, -k, 1),
        roll(v, k, 1),
    )


def weighted(coefs, v, k):
    terms = [m3(a, n) for a, n in zip(coefs, neighbours(v, k))]
    return (terms[0] + terms[1]) + (terms[2] + terms[3]) + (terms[4] + terms[5])


def pair_sum(v):
    rows, lanes = iota(v.shape, 0), iota(v.shape, 1)
    v = v + jnp.where(rows % 2 == 0, roll(v, -1, 0), roll(v, 1, 0))
    v = v + jnp.where(lanes % 32 < 16, roll(v, -16, 1), roll(v, 16, 1))
    return v + jnp.where(lanes % 2 == 0, roll(v, -1, 1), roll(v, 1, 1))


def edge_weights(s, k, scale):
    rows, lanes = iota(s.shape, 0), iota(s.shape, 1)
    coordinate = (rows, lanes // 16, lanes % 16)
    shifts = ((k, 0), (16 * k, 1), (k, 1))
    weights = []
    for where, (step, axis) in zip(coordinate, shifts):
        up = jnp.where(where < 16 - k, scale * (s + roll(s, -step, axis)), 0.0)
        low = jnp.where(where >= k, scale * (s + roll(s, step, axis)), 0.0)
        weights += [up, low]
    return weights, sum(weights[1:], weights[0])


def place(own, low):
    lane = iota((16, 128), 1)
    row = iota((16, 128), 0)
    inner = lane % 16
    parts = []
    for c in range(3):
        halves = []
        for h in range(2):
            r = 3 * h + c
            t = jnp.where(row == 15, own[r : r + 1, :], 0.0)
            t = t - jnp.where(row == 0, low[r : r + 1, :], 0.0)
            if h == 1:
                t = t + jnp.where(lane >= 112, roll(own[8:24], -16 - 16 * c, 1), 0.0)
            else:
                t = t - jnp.where(lane < 16, roll(low[8:24], -16 * c, 1), 0.0)
            t = t + jnp.where(inner == 15, roll(own[24:40], 15 - c - 3 * h, 1), 0.0)
            t = t - jnp.where(inner == 0, roll(low[24:40], -c - 3 * h, 1), 0.0)
            halves.append(t)
        parts.append(jnp.concatenate(halves, axis=1))
    return jnp.concatenate(parts, axis=0)


def pack_first(v, buf, high, lines=None):
    at = 15 if high else 0
    for c in range(3):
        row = v[16 * c + at : 16 * c + at + 1, :]
        if lines is not None:
            row = row + lines[c]
        buf[c : c + 1, :] = row[:, 0:128]
        buf[3 + c : 4 + c, :] = row[:, 128:256]
    buf[6:8, :] = jnp.zeros((2, 128), F32)


def pack_rest(v, buf, high):
    lane = iota((16, 128), 1)
    inner = lane % 16
    at = 15 if high else 0
    y = z = None
    for c in range(3):
        for h in range(2):
            part = v[16 * c : 16 * c + 16, 128 * h : 128 * h + 128]
            t = roll(jnp.where(inner == at, part, 0.0), c + 3 * h - at, 1)
            z = t if z is None else z + t
        if high:
            part = v[16 * c : 16 * c + 16, 128:256]
            t = roll(jnp.where(lane >= 112, part, 0.0), 16 + 16 * c, 1)
        else:
            part = v[16 * c : 16 * c + 16, 0:128]
            t = roll(jnp.where(lane < 16, part, 0.0), 16 * c, 1)
        y = t if y is None else y + t
    buf[8:24, :] = y
    buf[24:40, :] = z


def from_rows(rows, buf):
    lane = iota((16, 256), 1)
    row = iota((16, 256), 0)
    m, n = iota((256, 128), 0) % 16, iota((256, 128), 1)
    to_y = jnp.where(m == n % 16, 1.0, 0.0)
    to_z = jnp.where(n == (m % 8) * 16 + 3 * (m // 8), 1.0, 0.0)

    def spread(first):
        return jnp.concatenate(
            [jnp.where(lane // 16 == row, rows[first + c : first + c + 1, :], 0.0) for c in range(3)],
            axis=0,
        )

    y = jnp.dot(spread(3), to_y, precision=HI, preferred_element_type=F32)
    z = jnp.dot(spread(6), to_z, precision=HI, preferred_element_type=F32)
    group = iota((16, 128), 1) // 16
    buf[0:3, :] = rows[0:3, 0:128]
    buf[3:6, :] = rows[0:3, 128:256]
    buf[6:8, :] = jnp.zeros((2, 128), F32)
    buf[8:24, :] = sum(jnp.where(group == c, y[16 * c : 16 * c + 16], 0.0) for c in range(3))
    buf[24:40, :] = sum(roll(z[16 * c : 16 * c + 16], c, 1) for c in range(3))


def to_rows(faces, buf, slot):
    lane = iota((16, 256), 1)
    row = iota((16, 256), 0)
    n, m = iota((128, 256), 0), iota((128, 256), 1) % 16
    from_y = jnp.where(n == m, 1.0, 0.0)
    from_z = jnp.where(n == (m % 8) * 16 + 3 * (m // 8), 1.0, 0.0)
    y = jnp.concatenate([roll(faces[8:24], -16 * c, 1) for c in range(3)], axis=0)
    z = jnp.concatenate([roll(faces[24:40], -c, 1) for c in range(3)], axis=0)
    y = jnp.dot(y, from_y, precision=HI, preferred_element_type=F32)
    z = jnp.dot(z, from_z, precision=HI, preferred_element_type=F32)
    buf[slot, 0:3, 0:128] = faces[0:3]
    buf[slot, 0:3, 128:256] = faces[3:6]
    for c in range(3):
        for first, t in ((3, y), (6, z)):
            t = jnp.where(lane // 16 == row, t[16 * c : 16 * c + 16], 0.0)
            buf[slot, first + c : first + c + 1, :] = jnp.sum(t, axis=0, keepdims=True)


def partial_dot(a, b):
    t = jnp.sum(a * b, axis=0, keepdims=True)
    return t[:, 0:128] + t[:, 128:256]


def invert_columns(columns, row):
    for t in range(0, 8, 2):
        p, q = columns[t][t : t + 1], columns[t][t + 1 : t + 2]
        s = columns[t + 1][t + 1 : t + 2]
        d = 1.0 / p
        e = q * d
        p = 1.0 / (s - q * e)
        q = e * p
        s = d + e * q
        pair = (row == t) | (row == t + 1)
        c0 = jnp.where(pair, jnp.where(row == t, -1.0, 0.0), columns[t])
        c1 = jnp.where(pair, jnp.where(row == t, 0.0, -1.0), columns[t + 1])
        updated = []
        for j in range(8):
            if j == t:
                base, w0, w1 = 0.0, s, -q
            elif j == t + 1:
                base, w0, w1 = 0.0, -q, p
            else:
                a, b = columns[j][t : t + 1], columns[j][t + 1 : t + 2]
                base = jnp.where(pair, 0.0, columns[j])
                w0, w1 = s * a - q * b, p * b - q * a
            updated.append(base - c0 * w0 - c1 * w1)
        columns = updated
    return columns


def eliminate(matrix):
    count = matrix.shape[0] // 8
    row, lane = iota((8, 128), 0), iota((8, 128), 1)
    rows = [matrix[8 * i : 8 * i + 8, :] for i in range(count)]
    for k in range(count):
        pivot = rows[k]
        first = 8 * k
        columns = [
            jnp.broadcast_to(pivot[:, first + t : first + t + 1], (8, 128)) for t in range(8)
        ]
        inverse = invert_columns(columns, row)
        scaled = inverse[0] * pivot[0:1]
        for t in range(1, 8):
            scaled = scaled + inverse[t] * pivot[t : t + 1]
        for t in range(8):
            scaled = jnp.where(lane == first + t, inverse[t], scaled)
        hit = (lane >= first) & (lane < first + 8)
        for i in [(k + 1 + i) % count for i in range(count - 1)]:
            change = None
            for t in range(0, 8, 2):
                c0 = rows[i][:, first + t : first + t + 1]
                c1 = rows[i][:, first + t + 1 : first + t + 2]
                term = c0 * scaled[t : t + 1] + c1 * scaled[t + 1 : t + 2]
                change = term if change is None else change + term
            rows[i] = jnp.where(hit, 0.0, rows[i]) - change
        rows[k] = scaled
    for i in range(count):
        matrix[8 * i : 8 * i + 8, :] = rows[i]


def kernel(
    G, Y, Z, mult_hbm, res_hbm, class_hbm, moduli_hbm, panel_hbm, lam_ref, out_ref,
    mult_ref, res_ref, class_ref, moduli_ref, panel_ref, matrix, panel, sent_hi, sent_lo, got_hi,
    got_lo, corner_out, corner_in, tiles, x_in, sub_in, rows, load_sem, sum_sem, send_sem,
    recv_sem, far_sem,
):
    loads = [
        pltpu.make_async_copy(src, dst, load_sem.at[i])
        for i, (src, dst) in enumerate(
            (
                (res_hbm, res_ref),
                (panel_hbm, panel_ref),
                (class_hbm, class_ref),
                (mult_hbm, mult_ref),
                (moduli_hbm, moduli_ref),
            )
        )
    ]
    loads[0].start()

    sub, member = lax.axis_index("sub"), lax.axis_index("grp")
    n_sub = Y * Z * 2
    grid_row, grid_col = sub // SPAN, sub % SPAN
    upper = (
        ((sub + SPAN) % n_sub, member),
        (grid_row * SPAN + (grid_col + 1) % SPAN, member),
        (sub, (member + 1) % G),
    )
    lower = (
        ((sub + n_sub - SPAN) % n_sub, member),
        (grid_row * SPAN + (grid_col + SPAN - 1) % SPAN, member),
        (sub, (member + G - 1) % G),
    )
    upper_ok = [
        (grid_row < n_sub // SPAN - 1).astype(F32),
        (grid_col < SPAN - 1).astype(F32),
        (member < G - 1).astype(F32),
    ]
    lower_ok = [
        (grid_row > 0).astype(F32),
        (grid_col > 0).astype(F32),
        (member > 0).astype(F32),
    ]
    core, z, y = sub % 2, (sub // 2) % Z, sub // (2 * Z)
    by_distance = lambda n: sorted(range(1, n), key=lambda i: -min(i, n - i))
    x_partners = [(sub, (member + i) % G) for i in by_distance(G)]
    yc_partners = [
        (((y + i) % Y * Z + z) * 2 + (core + c) % 2, member)
        for i in by_distance(Y) + [0]
        for c in (1, 0)
        if (i, c) != (0, 0)
    ]
    along_z = lambda i: ((y * Z + (z + i) % Z) * 2 + core, member)
    distance = lambda o: min(o[0], Y - o[0]) + min(o[1], Z - o[1])
    offsets = [(i, j, c) for i in range(Y) for j in range(Z) for c in range(2)][1:]
    sub_partners = [
        (((y + i) % Y * Z + (z + j) % Z) * 2 + (core + c) % 2, member)
        for i, j, c in sorted(offsets, key=distance, reverse=True)
    ]

    barrier = pltpu.get_barrier_semaphore()
    greeted = [upper[0], lower[0], upper[1], lower[1]] + x_partners
    greeted += [p for p in yc_partners if p is not yc_partners[-1]]
    reach = min(2, Z // 2)
    greeted += [along_z(i) for n in range(1, reach + 1) for i in (n, Z - n)]
    for device in greeted:
        pl.semaphore_signal(barrier, inc=1, device_id=device, device_id_type=MESH)

    for load in loads[1:]:
        load.start()

    copies = []

    def send(src, dst, device):
        i = len(copies)
        copy = pltpu.make_async_remote_copy(
            src_ref=src, dst_ref=dst, send_sem=send_sem.at[i], recv_sem=recv_sem.at[i],
            device_id=device, device_id_type=MESH,
        )
        copy.start()
        copies.append(copy)
        return copy

    def wait(group):
        for copy in group:
            copy.wait_recv()

    spans = ((0, 8), (8, 24), (24, 40))

    def exchange(e, both=True, up=True, order=(0, 2, 1)):
        group = []
        for k in order:
            first, last = spans[k]
            if up:
                group.append(
                    send(sent_hi.at[e, first:last], got_hi.at[e, first:last], upper[k])
                )
            if both:
                group.append(
                    send(sent_lo.at[e, first:last], got_lo.at[e, first:last], lower[k])
                )
        return group

    face_row = iota((40, 128), 0)

    def face_mask(ok):
        return jnp.where(face_row < 8, ok[0], jnp.where(face_row < 24, ok[1], ok[2]))

    up_mask, low_mask = face_mask(upper_ok), face_mask(lower_ok)
    row9 = iota((9, 256), 0)
    row_mask = jnp.where(
        row9 < 3, upper_ok[0], jnp.where(row9 < 6, upper_ok[1], upper_ok[2])
    )

    size = G * CORNER
    own_rows = pl.ds(pl.multiple_of(member * CORNER, 8), CORNER)
    panel[...] = jnp.zeros((CORNER, 128), F32)
    loads[1].wait()
    panel[:, 0:size] = panel_ref[0]
    matrix[own_rows, :] = panel[...]

    loads[0].wait()
    residual = res_ref[:, 0, :] * row_mask
    from_rows(residual, sent_hi.at[0])
    rows[0] = residual

    loads[2].wait()
    loads[4].wait()
    classes = class_ref[0]
    stiffness = jnp.zeros((16, 256), F32)
    for level in range(8):
        stiffness = stiffness + jnp.where(classes == level, moduli_ref[level], 0.0)
    weight, total = edge_weights(stiffness, 1, 0.5)
    diagonal = 0.5 * stiffness + total
    scale = DAMP / diagonal
    relax = [scale * w for w in weight]
    block_mean = pair_sum(stiffness) * 0.125
    coarse_weight, coarse_total = edge_weights(block_mean, 2, 2.0)
    coarse_scale = DAMP / (4.0 * block_mean + coarse_total)
    coarse_relax = [coarse_scale * w for w in coarse_weight]

    def operator(v):
        return m3(diagonal, v) - weighted(weight, v, 1)

    def before_correction(f):
        g = m3(scale, f)
        v = (1.0 - DAMP) * g + g + weighted(relax, g, 1)
        defect = f - operator(v)
        h = m3(coarse_scale, pair_sum(defect))
        e = h
        for _ in range(3):
            e = (1.0 - DAMP) * e + h + weighted(coarse_relax, e, 2)
        return v, defect, v + e

    def after_correction(f, v):
        g = m3(scale, f)
        for _ in range(2):
            v = (1.0 - DAMP) * v + g + weighted(relax, v, 1)
        return v

    lanes = iota((1, 256), 1)
    ramp_y = (lanes // 16).astype(F32) / 15.0
    ramp_z = (lanes % 16).astype(F32) / 15.0
    plane = [
        by * bz for by in (1.0 - ramp_y, ramp_y) for bz in (1.0 - ramp_z, ramp_z)
    ]
    ramp_x = iota((16, 256), 0).astype(F32) / 15.0
    row8, lane8 = iota((8, 128), 0), iota((8, 128), 1)
    row8w = iota((8, 256), 0)
    plane8 = sum(jnp.where(row8w % 4 == n, plane[n], 0.0) for n in range(4))

    def corner_sums(f):
        t = jnp.zeros((8, 256), F32)
        for c in range(3):
            part = f[16 * c : 16 * c + 16]
            for a, ramp in ((0, 1.0 - ramp_x), (1, ramp_x)):
                line = jnp.sum(part * ramp, axis=0, keepdims=True)
                t = t + jnp.where(row8w == 2 * c + a, line, 0.0)
        result = jnp.zeros((8, 128), F32)
        for n in range(4):
            s = t * plane[n]
            s = jnp.sum(s[:, 0:128] + s[:, 128:256], axis=1, keepdims=True)
            at = (lane8 == member * CORNER + row8 * 4 + n) & (row8 < 6)
            result = result + jnp.where(at, s, 0.0)
        return jnp.sum(result, axis=0, keepdims=True)

    def corner_send(e, f):
        corner_out[e] = corner_sums(f)
        return [
            send(corner_out.at[e], corner_in.at[e, i], device)
            for i, device in enumerate(x_partners)
        ]

    def corner_rhs(e):
        rhs = corner_out[e]
        for i in range(G - 1):
            rhs = rhs + corner_in[e, i]
        return rhs

    lane1 = iota((1, 128), 1)

    def summed(products):
        t = jnp.zeros((8, 128), F32)
        for i, d in products:
            t = t + jnp.where(row8 == i, d, 0.0)
        t = jnp.sum(t, axis=1, keepdims=True)
        return jnp.sum(jnp.where(row8 == lane8, t, 0.0), axis=0, keepdims=True)

    row_m, lane_m = iota((size, 128), 0), iota((size, 128), 1)

    def as_column(line):
        return jnp.sum(jnp.where(row_m == lane_m, line, 0.0), axis=1, keepdims=True)

    def corner_lines(rhs):
        solved = jnp.sum(matrix[own_rows, :] * rhs, axis=1, keepdims=True)
        first, last = [], []
        for c in range(3):
            t = solved[8 * c : 8 * c + 8] * plane8
            first.append(jnp.sum(jnp.where(row8w < 4, t, 0.0), axis=0, keepdims=True))
            last.append(jnp.sum(jnp.where(row8w >= 4, t, 0.0), axis=0, keepdims=True))
        return first, last

    def corner_field(first, last):
        parts = [(1.0 - ramp_x) * a + ramp_x * b for a, b in zip(first, last)]
        return jnp.concatenate(parts, axis=0)

    def layers(e, v, corners=None):
        first, last = (None, None) if corners is None else corners
        pack_first(v, sent_hi.at[e], True, last)
        pack_first(v, sent_lo.at[e], False, first)
        group = exchange(e, order=(0,))
        if corners is not None:
            v = v + corner_field(first, last)
        pack_rest(v, sent_hi.at[e], True)
        pack_rest(v, sent_lo.at[e], False)
        return group + exchange(e, order=(2, 1)), v

    def far_signal(slot):
        step = min((1, 3, 4)[slot], Z // 2 - 1)
        for i in (step, Z - step):
            pl.semaphore_signal(
                far_sem.at[slot], inc=1, device_id=along_z(i), device_id_type=MESH
            )

    def far_wait(slot):
        pl.semaphore_wait(far_sem.at[slot], 2)

    pl.semaphore_wait(barrier, len(greeted))

    group = exchange(0, both=False)
    panels = [send(panel, matrix.at[own_rows, :], device) for device in x_partners]
    far_signal(0)
    wait(group)
    f_r = place(sent_hi[0], got_hi[0] * low_mask)

    image = operator(f_r)
    group, _ = layers(1, image)
    dots = [0.25 * partial_dot(f_r, image)]
    far_wait(0)
    far_signal(1)
    wait(panels)
    eliminate(matrix)
    wait(group)
    u = (sent_hi[1] - got_lo[1]) * (0.25 * up_mask)
    f_u = place(u, (got_hi[1] - sent_lo[1]) * (0.25 * low_mask))

    group = corner_send(0, f_u)
    _, defect_u, v = before_correction(f_u)
    v = after_correction(f_u, v)
    wait(group)
    rhs_u = corner_rhs(0)
    group, v = layers(2, v, corner_lines(rhs_u))
    dots.append(partial_dot(f_u, v))
    far_wait(1)
    far_signal(2)
    column_u = as_column(rhs_u)
    to_rows(u, rows, 1)
    wait(group)
    q = (sent_hi[2] - got_lo[2]) * up_mask
    f_q = place(q, (got_hi[2] - sent_lo[2]) * low_mask)

    image = operator(f_q)
    group, _ = layers(3, image)
    dots.append(0.25 * partial_dot(f_r, image))
    dots.append(0.25 * partial_dot(f_q, image))
    far_wait(2)
    early = summed(list(enumerate(dots)))
    to_rows(q, rows, 2)
    wait(group)
    w = (sent_hi[3] - got_lo[3]) * (0.25 * up_mask)
    f_w = place(w, (got_hi[3] - sent_lo[3]) * (0.25 * low_mask))

    corners = corner_send(1, f_w)
    before, defect_w, after = before_correction(f_w)
    tile = early + summed(
        [
            (4, partial_dot(f_u, before) + partial_dot(defect_u, after)),
            (5, partial_dot(f_w, before) + partial_dot(defect_w, after)),
        ]
    )
    tiles[0] = tile
    group = [
        send(tiles.at[0], x_in.at[i], device) for i, device in enumerate(x_partners)
    ]
    v = after_correction(f_w, after)
    wait(corners)
    rhs_w = corner_rhs(1)
    v = v + corner_field(*corner_lines(rhs_w))
    pack_first(v, sent_lo.at[4], False)
    pack_rest(v, sent_lo.at[4], False)
    last = exchange(4, up=False)
    solved_w = jnp.sum(matrix[...] * rhs_w, axis=1, keepdims=True)
    coarse_us = jnp.sum(column_u * solved_w, axis=0, keepdims=True)
    coarse_ws = jnp.sum(as_column(rhs_w) * solved_w, axis=0, keepdims=True)
    coarse = jnp.where(lane1 == 4, coarse_us, jnp.where(lane1 == 5, coarse_ws, 0.0))
    tile = tile + coarse
    wait(group)
    for i in range(G - 1):
        tile = tile + x_in[i]

    tiles[1] = tile
    for i, device in enumerate(sub_partners):
        pltpu.make_async_remote_copy(
            src_ref=tiles.at[1], dst_ref=sub_in.at[i], send_sem=sum_sem.at[0],
            recv_sem=sum_sem.at[1], device_id=device, device_id_type=MESH,
        ).start()
    arrived = pltpu.make_async_remote_copy(
        src_ref=sub_in, dst_ref=sub_in, send_sem=sum_sem.at[0], recv_sem=sum_sem.at[1],
        device_id=sub_partners[0], device_id_type=MESH,
    )
    pack_first(v, sent_hi.at[4], True)
    pack_rest(v, sent_hi.at[4], True)
    to_rows(w, rows, 3)
    wait(last)
    to_rows((sent_hi[4] - got_lo[4]) * up_mask, rows, 4)
    loads[3].wait()
    for copy in copies:
        copy.wait_send()
    arrived.wait_recv()
    parts = [sub_in[i] for i in range(len(sub_partners))] + [tile]
    while len(parts) > 1:
        parts = [sum(parts[i : i + 2][1:], parts[i]) for i in range(0, len(parts), 2)]
    tile = parts[0]
    arrived.wait_send()

    ru, uq, rw, qw, us, ws = [tile[:, i : i + 1] for i in range(6)]
    a = ru / uq
    next_inner = ru - a * (rw + uq) + a * a * qw
    c = 1.0 + next_inner / ru
    curve = c * c * uq - c * a * (us + qw) + a * a * ws
    b = next_inner / curve
    first, second = a + b * c, a * b
    lam_ref[:, 0, :] = mult_ref[:, 0, :] * row_mask + first * rows[1] - second * rows[3]
    out_ref[:, 0, :] = rows[0] - first * rows[2] + second * rows[4]


def deliver(lam_ref, out_ref, lam_hbm, out_hbm, sem):
    copies = [
        pltpu.make_async_copy(lam_ref, lam_hbm, sem.at[0]),
        pltpu.make_async_copy(out_ref, out_hbm, sem.at[1]),
    ]
    for copy in copies:
        copy.start()
    for copy in copies:
        copy.wait()


def solution(mesh):
    G, n_sub = mesh.shape["grp"], mesh.shape["sub"]
    Z = min(16, n_sub // 2)
    Y = n_sub // (2 * Z)
    size = G * CORNER
    copies = 3 + 3 * 6 + 3 + 4 * (G - 1)

    def per_device(multipliers, residual, stiff_class, moduli, coarse_panel):
        vmem = pl.BlockSpec(memory_space=pltpu.VMEM)
        hbm = pl.BlockSpec(memory_space=pltpu.HBM)
        face_first = (1, 0, 2)
        in_hbm = lambda x: pltpu.with_memory_space_constraint(x, pltpu.HBM)
        lam, out = pl.pallas_call(
            functools.partial(kernel, G, Y, Z),
            out_shape=[jax.ShapeDtypeStruct((9, 1, 256), F32)] * 2,
            in_specs=[hbm] * 5,
            out_specs=[vmem, vmem],
            scratch_shapes=[
                pltpu.VMEM((9, 1, 256), F32),
                pltpu.VMEM((9, 1, 256), F32),
                pltpu.VMEM((1, 16, 256), jnp.int32),
                pltpu.SMEM((8,), F32),
                pltpu.VMEM((1, CORNER, size), F32),
                pltpu.VMEM((size, 128), F32),
                pltpu.VMEM((CORNER, 128), F32),
                pltpu.VMEM((5, 40, 128), F32),
                pltpu.VMEM((5, 40, 128), F32),
                pltpu.VMEM((5, 40, 128), F32),
                pltpu.VMEM((5, 40, 128), F32),
                pltpu.VMEM((2, 1, 128), F32),
                pltpu.VMEM((2, G - 1, 1, 128), F32),
                pltpu.VMEM((2, 1, 128), F32),
                pltpu.VMEM((G - 1, 1, 128), F32),
                pltpu.VMEM((n_sub - 1, 1, 128), F32),
                pltpu.VMEM((5, 9, 256), F32),
                pltpu.SemaphoreType.DMA((5,)),
                pltpu.SemaphoreType.DMA((2,)),
                pltpu.SemaphoreType.DMA((copies,)),
                pltpu.SemaphoreType.DMA((copies,)),
                pltpu.SemaphoreType.REGULAR((3,)),
            ],
            compiler_params=pltpu.CompilerParams(
                collective_id=0, has_side_effects=True, vmem_limit_bytes=32 * 1024 * 1024
            ),
            name="feti",
        )(
            in_hbm(multipliers.transpose(face_first)),
            in_hbm(residual.transpose(face_first)),
            in_hbm(stiff_class),
            in_hbm(moduli),
            in_hbm(coarse_panel),
        )
        lam, out = pl.pallas_call(
            deliver,
            out_shape=[jax.ShapeDtypeStruct((9, 1, 256), F32)] * 2,
            in_specs=[vmem, vmem],
            out_specs=[hbm, hbm],
            scratch_shapes=[pltpu.SemaphoreType.DMA((2,))],
            compiler_params=pltpu.CompilerParams(vmem_limit_bytes=1024 * 1024),
            name="deliver",
        )(lam, out)
        return lam.transpose(face_first), out.transpose(face_first)

    device = P(("sub", "grp"), None, None)
    return jax.shard_map(
        per_device,
        mesh=mesh,
        in_specs=(device, device, device, P(), device),
        out_specs=(device, device),
        check_vma=False,
    )
```

```python
import functools

import jax
import jax.numpy as jnp
from jax import lax
from jax.experimental import pallas as pl
from jax.experimental.pallas import tpu as pltpu
from jax.sharding import PartitionSpec as P

MESH = pl.DeviceIdType.MESH
F32 = jnp.float32
SPAN = 4
CORNER = 24
DAMP = 0.8
HI = lax.Precision.HIGHEST


def roll(x, shift, axis):
    shift = shift % x.shape[axis]
    return x if shift == 0 else pltpu.roll(x, shift, axis)


def iota(shape, axis):
    return lax.broadcasted_iota(jnp.int32, shape, axis)


def m3(coef, field):
    return (field.reshape(3, 16, 256) * coef[None]).reshape(48, 256)


def neighbours(v, k):
    return (
        roll(v, -k, 0),
        roll(v, k, 0),
        roll(v, -16 * k, 1),
        roll(v, 16 * k, 1),
        roll(v, -k, 1),
        roll(v, k, 1),
    )


def weighted(coefs, v, k):
    terms = [m3(a, n) for a, n in zip(coefs, neighbours(v, k))]
    return (terms[0] + terms[1]) + (terms[2] + terms[3]) + (terms[4] + terms[5])


def pair_sum(v):
    rows, lanes = iota(v.shape, 0), iota(v.shape, 1)
    v = v + jnp.where(rows % 2 == 0, roll(v, -1, 0), roll(v, 1, 0))
    v = v + jnp.where(lanes % 32 < 16, roll(v, -16, 1), roll(v, 16, 1))
    return v + jnp.where(lanes % 2 == 0, roll(v, -1, 1), roll(v, 1, 1))


def edge_weights(s, k, scale):
    rows, lanes = iota(s.shape, 0), iota(s.shape, 1)
    coordinate = (rows, lanes // 16, lanes % 16)
    shifts = ((k, 0), (16 * k, 1), (k, 1))
    weights = []
    for where, (step, axis) in zip(coordinate, shifts):
        up = jnp.where(where < 16 - k, scale * (s + roll(s, -step, axis)), 0.0)
        low = jnp.where(where >= k, scale * (s + roll(s, step, axis)), 0.0)
        weights += [up, low]
    return weights, sum(weights[1:], weights[0])


def place(own, low):
    lane = iota((16, 128), 1)
    row = iota((16, 128), 0)
    inner = lane % 16
    parts = []
    for c in range(3):
        halves = []
        for h in range(2):
            r = 3 * h + c
            t = jnp.where(row == 15, own[r : r + 1, :], 0.0)
            t = t - jnp.where(row == 0, low[r : r + 1, :], 0.0)
            if h == 1:
                t = t + jnp.where(lane >= 112, roll(own[8:24], -16 - 16 * c, 1), 0.0)
            else:
                t = t - jnp.where(lane < 16, roll(low[8:24], -16 * c, 1), 0.0)
            t = t + jnp.where(inner == 15, roll(own[24:40], 15 - c - 3 * h, 1), 0.0)
            t = t - jnp.where(inner == 0, roll(low[24:40], -c - 3 * h, 1), 0.0)
            halves.append(t)
        parts.append(jnp.concatenate(halves, axis=1))
    return jnp.concatenate(parts, axis=0)


def pack_first(v, buf, high, lines=None):
    at = 15 if high else 0
    for c in range(3):
        row = v[16 * c + at : 16 * c + at + 1, :]
        if lines is not None:
            row = row + lines[c]
        buf[c : c + 1, :] = row[:, 0:128]
        buf[3 + c : 4 + c, :] = row[:, 128:256]
    buf[6:8, :] = jnp.zeros((2, 128), F32)


def pack_rest(v, buf, high):
    lane = iota((16, 128), 1)
    inner = lane % 16
    at = 15 if high else 0
    y = z = None
    for c in range(3):
        for h in range(2):
            part = v[16 * c : 16 * c + 16, 128 * h : 128 * h + 128]
            t = roll(jnp.where(inner == at, part, 0.0), c + 3 * h - at, 1)
            z = t if z is None else z + t
        if high:
            part = v[16 * c : 16 * c + 16, 128:256]
            t = roll(jnp.where(lane >= 112, part, 0.0), 16 + 16 * c, 1)
        else:
            part = v[16 * c : 16 * c + 16, 0:128]
            t = roll(jnp.where(lane < 16, part, 0.0), 16 * c, 1)
        y = t if y is None else y + t
    buf[8:24, :] = y
    buf[24:40, :] = z


def from_rows(rows, buf):
    lane = iota((16, 256), 1)
    row = iota((16, 256), 0)
    m, n = iota((256, 128), 0) % 16, iota((256, 128), 1)
    to_y = jnp.where(m == n % 16, 1.0, 0.0)
    to_z = jnp.where(n == (m % 8) * 16 + 3 * (m // 8), 1.0, 0.0)

    def spread(first):
        return jnp.concatenate(
            [jnp.where(lane // 16 == row, rows[first + c : first + c + 1, :], 0.0) for c in range(3)],
            axis=0,
        )

    y = jnp.dot(spread(3), to_y, precision=HI, preferred_element_type=F32)
    z = jnp.dot(spread(6), to_z, precision=HI, preferred_element_type=F32)
    group = iota((16, 128), 1) // 16
    buf[0:3, :] = rows[0:3, 0:128]
    buf[3:6, :] = rows[0:3, 128:256]
    buf[6:8, :] = jnp.zeros((2, 128), F32)
    buf[8:24, :] = sum(jnp.where(group == c, y[16 * c : 16 * c + 16], 0.0) for c in range(3))
    buf[24:40, :] = sum(roll(z[16 * c : 16 * c + 16], c, 1) for c in range(3))


def to_rows(faces, buf, slot):
    lane = iota((16, 256), 1)
    row = iota((16, 256), 0)
    n, m = iota((128, 256), 0), iota((128, 256), 1) % 16
    from_y = jnp.where(n == m, 1.0, 0.0)
    from_z = jnp.where(n == (m % 8) * 16 + 3 * (m // 8), 1.0, 0.0)
    y = jnp.concatenate([roll(faces[8:24], -16 * c, 1) for c in range(3)], axis=0)
    z = jnp.concatenate([roll(faces[24:40], -c, 1) for c in range(3)], axis=0)
    y = jnp.dot(y, from_y, precision=HI, preferred_element_type=F32)
    z = jnp.dot(z, from_z, precision=HI, preferred_element_type=F32)
    buf[slot, 0:3, 0:128] = faces[0:3]
    buf[slot, 0:3, 128:256] = faces[3:6]
    for c in range(3):
        for first, t in ((3, y), (6, z)):
            t = jnp.where(lane // 16 == row, t[16 * c : 16 * c + 16], 0.0)
            buf[slot, first + c : first + c + 1, :] = jnp.sum(t, axis=0, keepdims=True)


def partial_dot(a, b):
    t = jnp.sum(a * b, axis=0, keepdims=True)
    return t[:, 0:128] + t[:, 128:256]


def invert_columns(columns, row):
    for t in range(0, 8, 2):
        p, q = columns[t][t : t + 1], columns[t][t + 1 : t + 2]
        s = columns[t + 1][t + 1 : t + 2]
        d = 1.0 / p
        e = q * d
        p = 1.0 / (s - q * e)
        q = e * p
        s = d + e * q
        pair = (row == t) | (row == t + 1)
        c0 = jnp.where(pair, jnp.where(row == t, -1.0, 0.0), columns[t])
        c1 = jnp.where(pair, jnp.where(row == t, 0.0, -1.0), columns[t + 1])
        updated = []
        for j in range(8):
            if j == t:
                base, w0, w1 = 0.0, s, -q
            elif j == t + 1:
                base, w0, w1 = 0.0, -q, p
            else:
                a, b = columns[j][t : t + 1], columns[j][t + 1 : t + 2]
                base = jnp.where(pair, 0.0, columns[j])
                w0, w1 = s * a - q * b, p * b - q * a
            updated.append(base - c0 * w0 - c1 * w1)
        columns = updated
    return columns


def eliminate(matrix):
    count = matrix.shape[0] // 8
    row, lane = iota((8, 128), 0), iota((8, 128), 1)
    rows = [matrix[8 * i : 8 * i + 8, :] for i in range(count)]
    for k in range(count):
        pivot = rows[k]
        first = 8 * k
        columns = [
            jnp.broadcast_to(pivot[:, first + t : first + t + 1], (8, 128)) for t in range(8)
        ]
        inverse = invert_columns(columns, row)
        scaled = inverse[0] * pivot[0:1]
        for t in range(1, 8):
            scaled = scaled + inverse[t] * pivot[t : t + 1]
        for t in range(8):
            scaled = jnp.where(lane == first + t, inverse[t], scaled)
        hit = (lane >= first) & (lane < first + 8)
        for i in [(k + 1 + i) % count for i in range(count - 1)]:
            change = None
            for t in range(0, 8, 2):
                c0 = rows[i][:, first + t : first + t + 1]
                c1 = rows[i][:, first + t + 1 : first + t + 2]
                term = c0 * scaled[t : t + 1] + c1 * scaled[t + 1 : t + 2]
                change = term if change is None else change + term
            rows[i] = jnp.where(hit, 0.0, rows[i]) - change
        rows[k] = scaled
    for i in range(count):
        matrix[8 * i : 8 * i + 8, :] = rows[i]


def kernel(
    G, Y, Z, mult_hbm, res_hbm, class_hbm, moduli_hbm, panel_hbm, lam_ref, out_ref,
    mult_ref, res_ref, class_ref, moduli_ref, panel_ref, matrix, panel, sent_hi, sent_lo, got_hi,
    got_lo, corner_out, corner_in, tiles, x_in, sub_in, rows, load_sem, sum_sem, send_sem,
    recv_sem, far_sem,
):
    loads = [
        pltpu.make_async_copy(src, dst, load_sem.at[i])
        for i, (src, dst) in enumerate(
            (
                (res_hbm, res_ref),
                (panel_hbm, panel_ref),
                (class_hbm, class_ref),
                (mult_hbm, mult_ref),
                (moduli_hbm, moduli_ref),
            )
        )
    ]
    loads[0].start()

    sub, member = lax.axis_index("sub"), lax.axis_index("grp")
    n_sub = Y * Z * 2
    grid_row, grid_col = sub // SPAN, sub % SPAN
    upper = (
        ((sub + SPAN) % n_sub, member),
        (grid_row * SPAN + (grid_col + 1) % SPAN, member),
        (sub, (member + 1) % G),
    )
    lower = (
        ((sub + n_sub - SPAN) % n_sub, member),
        (grid_row * SPAN + (grid_col + SPAN - 1) % SPAN, member),
        (sub, (member + G - 1) % G),
    )
    upper_ok = [
        (grid_row < n_sub // SPAN - 1).astype(F32),
        (grid_col < SPAN - 1).astype(F32),
        (member < G - 1).astype(F32),
    ]
    lower_ok = [
        (grid_row > 0).astype(F32),
        (grid_col > 0).astype(F32),
        (member > 0).astype(F32),
    ]
    core, z, y = sub % 2, (sub // 2) % Z, sub // (2 * Z)
    by_distance = lambda n: sorted(range(1, n), key=lambda i: -min(i, n - i))
    x_partners = [(sub, (member + i) % G) for i in by_distance(G)]
    yc_partners = [
        (((y + i) % Y * Z + z) * 2 + (core + c) % 2, member)
        for i in by_distance(Y) + [0]
        for c in (1, 0)
        if (i, c) != (0, 0)
    ]
    along_z = lambda i: ((y * Z + (z + i) % Z) * 2 + core, member)
    distance = lambda o: min(o[0], Y - o[0]) + min(o[1], Z - o[1])
    offsets = [(i, j, c) for i in range(Y) for j in range(Z) for c in range(2)][1:]
    sub_partners = [
        (((y + i) % Y * Z + (z + j) % Z) * 2 + (core + c) % 2, member)
        for i, j, c in sorted(offsets, key=distance, reverse=True)
    ]

    barrier = pltpu.get_barrier_semaphore()
    greeted = [upper[0], lower[0], upper[1], lower[1]] + x_partners
    greeted += [p for p in yc_partners if p is not yc_partners[-1]]
    reach = min(2, Z // 2)
    greeted += [along_z(i) for n in range(1, reach + 1) for i in (n, Z - n)]
    for device in greeted:
        pl.semaphore_signal(barrier, inc=1, device_id=device, device_id_type=MESH)

    for load in loads[1:]:
        load.start()

    copies = []

    def send(src, dst, device):
        i = len(copies)
        copy = pltpu.make_async_remote_copy(
            src_ref=src, dst_ref=dst, send_sem=send_sem.at[i], recv_sem=recv_sem.at[i],
            device_id=device, device_id_type=MESH,
        )
        copy.start()
        copies.append(copy)
        return copy

    def wait(group):
        for copy in group:
            copy.wait_recv()

    spans = ((0, 8), (8, 24), (24, 40))

    def exchange(e, both=True, up=True, order=(0, 2, 1)):
        group = []
        for k in order:
            first, last = spans[k]
            if up:
                group.append(
                    send(sent_hi.at[e, first:last], got_hi.at[e, first:last], upper[k])
                )
            if both:
                group.append(
                    send(sent_lo.at[e, first:last], got_lo.at[e, first:last], lower[k])
                )
        return group

    face_row = iota((40, 128), 0)

    def face_mask(ok):
        return jnp.where(face_row < 8, ok[0], jnp.where(face_row < 24, ok[1], ok[2]))

    up_mask, low_mask = face_mask(upper_ok), face_mask(lower_ok)
    row9 = iota((9, 256), 0)
    row_mask = jnp.where(
        row9 < 3, upper_ok[0], jnp.where(row9 < 6, upper_ok[1], upper_ok[2])
    )

    size = G * CORNER
    own_rows = pl.ds(pl.multiple_of(member * CORNER, 8), CORNER)
    panel[...] = jnp.zeros((CORNER, 128), F32)
    loads[1].wait()
    panel[:, 0:size] = panel_ref[0]
    matrix[own_rows, :] = panel[...]

    loads[0].wait()
    residual = res_ref[:, 0, :] * row_mask
    from_rows(residual, sent_hi.at[0])
    rows[0] = residual

    loads[2].wait()
    loads[4].wait()
    classes = class_ref[0]
    stiffness = jnp.zeros((16, 256), F32)
    for level in range(8):
        stiffness = stiffness + jnp.where(classes == level, moduli_ref[level], 0.0)
    weight, total = edge_weights(stiffness, 1, 0.5)
    diagonal = 0.5 * stiffness + total
    scale = DAMP / diagonal
    relax = [scale * w for w in weight]
    block_mean = pair_sum(stiffness) * 0.125
    coarse_weight, coarse_total = edge_weights(block_mean, 2, 2.0)
    coarse_scale = DAMP / (4.0 * block_mean + coarse_total)
    coarse_relax = [coarse_scale * w for w in coarse_weight]

    def operator(v):
        return m3(diagonal, v) - weighted(weight, v, 1)

    def before_correction(f):
        g = m3(scale, f)
        v = (1.0 - DAMP) * g + g + weighted(relax, g, 1)
        defect = f - operator(v)
        h = m3(coarse_scale, pair_sum(defect))
        e = h
        for _ in range(3):
            e = (1.0 - DAMP) * e + h + weighted(coarse_relax, e, 2)
        return v, defect, v + e

    def after_correction(f, v):
        g = m3(scale, f)
        for _ in range(2):
            v = (1.0 - DAMP) * v + g + weighted(relax, v, 1)
        return v

    lanes = iota((1, 256), 1)
    ramp_y = (lanes // 16).astype(F32) / 15.0
    ramp_z = (lanes % 16).astype(F32) / 15.0
    plane = [
        by * bz for by in (1.0 - ramp_y, ramp_y) for bz in (1.0 - ramp_z, ramp_z)
    ]
    ramp_x = iota((16, 256), 0).astype(F32) / 15.0
    row8, lane8 = iota((8, 128), 0), iota((8, 128), 1)
    row8w = iota((8, 256), 0)
    plane8 = sum(jnp.where(row8w % 4 == n, plane[n], 0.0) for n in range(4))

    def corner_sums(f):
        t = jnp.zeros((8, 256), F32)
        for c in range(3):
            part = f[16 * c : 16 * c + 16]
            for a, ramp in ((0, 1.0 - ramp_x), (1, ramp_x)):
                line = jnp.sum(part * ramp, axis=0, keepdims=True)
                t = t + jnp.where(row8w == 2 * c + a, line, 0.0)
        result = jnp.zeros((8, 128), F32)
        for n in range(4):
            s = t * plane[n]
            s = jnp.sum(s[:, 0:128] + s[:, 128:256], axis=1, keepdims=True)
            at = (lane8 == member * CORNER + row8 * 4 + n) & (row8 < 6)
            result = result + jnp.where(at, s, 0.0)
        return jnp.sum(result, axis=0, keepdims=True)

    def corner_send(e, f):
        corner_out[e] = corner_sums(f)
        return [
            send(corner_out.at[e], corner_in.at[e, i], device)
            for i, device in enumerate(x_partners)
        ]

    def corner_rhs(e):
        rhs = corner_out[e]
        for i in range(G - 1):
            rhs = rhs + corner_in[e, i]
        return rhs

    lane1 = iota((1, 128), 1)

    def summed(products):
        t = jnp.zeros((8, 128), F32)
        for i, d in products:
            t = t + jnp.where(row8 == i, d, 0.0)
        t = jnp.sum(t, axis=1, keepdims=True)
        return jnp.sum(jnp.where(row8 == lane8, t, 0.0), axis=0, keepdims=True)

    row_m, lane_m = iota((size, 128), 0), iota((size, 128), 1)

    def as_column(line):
        return jnp.sum(jnp.where(row_m == lane_m, line, 0.0), axis=1, keepdims=True)

    def corner_lines(rhs):
        solved = jnp.sum(matrix[own_rows, :] * rhs, axis=1, keepdims=True)
        first, last = [], []
        for c in range(3):
            t = solved[8 * c : 8 * c + 8] * plane8
            first.append(jnp.sum(jnp.where(row8w < 4, t, 0.0), axis=0, keepdims=True))
            last.append(jnp.sum(jnp.where(row8w >= 4, t, 0.0), axis=0, keepdims=True))
        return first, last

    def corner_field(first, last):
        parts = [(1.0 - ramp_x) * a + ramp_x * b for a, b in zip(first, last)]
        return jnp.concatenate(parts, axis=0)

    def layers(e, v, corners=None):
        first, last = (None, None) if corners is None else corners
        pack_first(v, sent_hi.at[e], True, last)
        pack_first(v, sent_lo.at[e], False, first)
        group = exchange(e, order=(0,))
        if corners is not None:
            v = v + corner_field(first, last)
        pack_rest(v, sent_hi.at[e], True)
        pack_rest(v, sent_lo.at[e], False)
        return group + exchange(e, order=(2, 1)), v

    def far_signal(slot):
        step = min((1, 3, 4)[slot], Z // 2 - 1)
        for i in (step, Z - step):
            pl.semaphore_signal(
                far_sem.at[slot], inc=1, device_id=along_z(i), device_id_type=MESH
            )

    def far_wait(slot):
        pl.semaphore_wait(far_sem.at[slot], 2)

    pl.semaphore_wait(barrier, len(greeted))

    group = exchange(0, both=False)
    panels = [send(panel, matrix.at[own_rows, :], device) for device in x_partners]
    far_signal(0)
    wait(group)
    f_r = place(sent_hi[0], got_hi[0] * low_mask)

    image = operator(f_r)
    group, _ = layers(1, image)
    dots = [0.25 * partial_dot(f_r, image)]
    far_wait(0)
    far_signal(1)
    wait(panels)
    eliminate(matrix)
    wait(group)
    u = (sent_hi[1] - got_lo[1]) * (0.25 * up_mask)
    f_u = place(u, (got_hi[1] - sent_lo[1]) * (0.25 * low_mask))

    group = corner_send(0, f_u)
    _, _, v = before_correction(f_u)
    v = after_correction(f_u, v)
    wait(group)
    rhs_u = corner_rhs(0)
    group, v = layers(2, v, corner_lines(rhs_u))
    dots.append(partial_dot(f_u, v))
    far_wait(1)
    far_signal(2)
    to_rows(u, rows, 1)
    wait(group)
    q = (sent_hi[2] - got_lo[2]) * up_mask
    f_q = place(q, (got_hi[2] - sent_lo[2]) * low_mask)

    image = operator(f_q)
    group, _ = layers(3, image)
    dots.append(0.25 * partial_dot(f_r, image))
    dots.append(0.25 * partial_dot(f_q, image))
    far_wait(2)
    early = summed(list(enumerate(dots)))
    to_rows(q, rows, 2)
    wait(group)
    w = (sent_hi[3] - got_lo[3]) * (0.25 * up_mask)
    f_w = place(w, (got_hi[3] - sent_lo[3]) * (0.25 * low_mask))

    corners = corner_send(1, f_w)
    before, defect_w, after = before_correction(f_w)
    tile = early + summed(
        [
            (4, jnp.sum(q * w, axis=0, keepdims=True)),
            (5, partial_dot(f_w, before) + partial_dot(defect_w, after)),
        ]
    )
    tiles[0] = tile
    group = [
        send(tiles.at[0], x_in.at[i], device) for i, device in enumerate(x_partners)
    ]
    v = after_correction(f_w, after)
    wait(corners)
    rhs_w = corner_rhs(1)
    solved_w = jnp.sum(matrix[...] * rhs_w, axis=1, keepdims=True)
    coarse_ws = jnp.sum(as_column(rhs_w) * solved_w, axis=0, keepdims=True)
    tile = tile + jnp.where(lane1 == 5, coarse_ws, 0.0)
    wait(group)
    for i in range(G - 1):
        tile = tile + x_in[i]

    tiles[1] = tile
    for i, device in enumerate(sub_partners):
        if i == len(sub_partners) // 4:
            v = v + corner_field(*corner_lines(rhs_w))
            pack_first(v, sent_lo.at[4], False)
            pack_rest(v, sent_lo.at[4], False)
            last = exchange(4, up=False)
        pltpu.make_async_remote_copy(
            src_ref=tiles.at[1], dst_ref=sub_in.at[i], send_sem=sum_sem.at[0],
            recv_sem=sum_sem.at[1], device_id=device, device_id_type=MESH,
        ).start()
    arrived = pltpu.make_async_remote_copy(
        src_ref=sub_in, dst_ref=sub_in, send_sem=sum_sem.at[0], recv_sem=sum_sem.at[1],
        device_id=sub_partners[0], device_id_type=MESH,
    )
    pack_first(v, sent_hi.at[4], True)
    pack_rest(v, sent_hi.at[4], True)
    to_rows(w, rows, 3)
    wait(last)
    to_rows((sent_hi[4] - got_lo[4]) * up_mask, rows, 4)
    loads[3].wait()
    for copy in copies:
        copy.wait_send()
    arrived.wait_recv()
    parts = [sub_in[i] for i in range(len(sub_partners))] + [tile]
    while len(parts) > 1:
        parts = [sum(parts[i : i + 2][1:], parts[i]) for i in range(0, len(parts), 2)]
    tile = parts[0]
    arrived.wait_send()

    ru, uq, rw, qw, us, ws = [tile[:, i : i + 1] for i in range(6)]
    a = ru / uq
    next_inner = ru - a * (rw + uq) + a * a * qw
    c = 1.0 + next_inner / ru
    curve = c * c * uq - c * a * (us + qw) + a * a * ws
    b = next_inner / curve
    first, second = a + b * c, a * b
    lam_ref[:, 0, :] = mult_ref[:, 0, :] * row_mask + first * rows[1] - second * rows[3]
    out_ref[:, 0, :] = rows[0] - first * rows[2] + second * rows[4]


def deliver(lam_ref, out_ref, lam_hbm, out_hbm, sem):
    copies = [
        pltpu.make_async_copy(lam_ref, lam_hbm, sem.at[0]),
        pltpu.make_async_copy(out_ref, out_hbm, sem.at[1]),
    ]
    for copy in copies:
        copy.start()
    for copy in copies:
        copy.wait()


def solution(mesh):
    G, n_sub = mesh.shape["grp"], mesh.shape["sub"]
    Z = min(16, n_sub // 2)
    Y = n_sub // (2 * Z)
    size = G * CORNER
    copies = 3 + 3 * 6 + 3 + 4 * (G - 1)

    def per_device(multipliers, residual, stiff_class, moduli, coarse_panel):
        vmem = pl.BlockSpec(memory_space=pltpu.VMEM)
        hbm = pl.BlockSpec(memory_space=pltpu.HBM)
        face_first = (1, 0, 2)
        in_hbm = lambda x: pltpu.with_memory_space_constraint(x, pltpu.HBM)
        lam, out = pl.pallas_call(
            functools.partial(kernel, G, Y, Z),
            out_shape=[jax.ShapeDtypeStruct((9, 1, 256), F32)] * 2,
            in_specs=[hbm] * 5,
            out_specs=[vmem, vmem],
            scratch_shapes=[
                pltpu.VMEM((9, 1, 256), F32),
                pltpu.VMEM((9, 1, 256), F32),
                pltpu.VMEM((1, 16, 256), jnp.int32),
                pltpu.SMEM((8,), F32),
                pltpu.VMEM((1, CORNER, size), F32),
                pltpu.VMEM((size, 128), F32),
                pltpu.VMEM((CORNER, 128), F32),
                pltpu.VMEM((5, 40, 128), F32),
                pltpu.VMEM((5, 40, 128), F32),
                pltpu.VMEM((5, 40, 128), F32),
                pltpu.VMEM((5, 40, 128), F32),
                pltpu.VMEM((2, 1, 128), F32),
                pltpu.VMEM((2, G - 1, 1, 128), F32),
                pltpu.VMEM((2, 1, 128), F32),
                pltpu.VMEM((G - 1, 1, 128), F32),
                pltpu.VMEM((n_sub - 1, 1, 128), F32),
                pltpu.VMEM((5, 9, 256), F32),
                pltpu.SemaphoreType.DMA((5,)),
                pltpu.SemaphoreType.DMA((2,)),
                pltpu.SemaphoreType.DMA((copies,)),
                pltpu.SemaphoreType.DMA((copies,)),
                pltpu.SemaphoreType.REGULAR((3,)),
            ],
            compiler_params=pltpu.CompilerParams(
                collective_id=0, has_side_effects=True, vmem_limit_bytes=32 * 1024 * 1024
            ),
            name="feti",
        )(
            in_hbm(multipliers.transpose(face_first)),
            in_hbm(residual.transpose(face_first)),
            in_hbm(stiff_class),
            in_hbm(moduli),
            in_hbm(coarse_panel),
        )
        lam, out = pl.pallas_call(
            deliver,
            out_shape=[jax.ShapeDtypeStruct((9, 1, 256), F32)] * 2,
            in_specs=[vmem, vmem],
            out_specs=[hbm, hbm],
            scratch_shapes=[pltpu.SemaphoreType.DMA((2,))],
            compiler_params=pltpu.CompilerParams(vmem_limit_bytes=1024 * 1024),
            name="deliver",
        )(lam, out)
        return lam.transpose(face_first), out.transpose(face_first)

    device = P(("sub", "grp"), None, None)
    return jax.shard_map(
        per_device,
        mesh=mesh,
        in_specs=(device, device, device, P(), device),
        out_specs=(device, device),
        check_vma=False,
    )
```
